32 devices in a mesh: groups: 2 (over x), dp: 8 (over z, y), tile: 2 (over core).
Axes of the slice: x: 2, y: 2, z: 4, core: 2. Of those that a mesh axis runs over, the one named last changes fastest.
Arguments:
- coords: bfloat16 [80512, 3, 256], P(('groups', 'dp', 'tile')), parts along dimension 0, may hold values from -4 to 4
- lengths: int32 [32], P('groups'), parts along dimension 0, may hold values from 501 to 2516, as said below
- atom_pairs: int32 [2, 1024], replicated, may hold values from 0 to 255, as said below
Outputs:
- cov_zero: float32 [2048, 1024], P(('groups', 'dp'), 'tile'), parts along dimension 0
- cov_lag: float32 [2048, 1024], P(('groups', 'dp'), 'tile'), parts along dimension 0
The draws below stay inside these ranges and needn't reach their ends.
There are 2 independent parts, one for each index of `groups`. The reference program is written for one: setup_inputs(seed, part) draws one part's arguments, and reference() takes and returns one part's arrays. A program takes and returns all parts, laid end to end along the dimension named above; an argument that names none is the same for every part. Nothing has to cross between parts.
Inputs may be any that keep to these rules, and one draw needn't show every extreme that they name: `lengths`: each trajectory's pair starts, grouped 32 to a block from its first frame, fill 1 to 63 blocks; all trajectories together fill exactly 512 blocks, and one fills 63. `atom_pairs`: each feature names two different atoms.
All inputs are finite; a program needn't handle non-finite values.
Results may differ from the reference program's by a relative error of at most 0.00045.
Values may be sent and summed in bfloat16 or wider, within the bound.
No kernel may reach another device: no remote copies, remote signals or barrier semaphores. Data moves between devices by JAX's collectives and lax.ppermute only.
A program may use at most 128 MiB of HBM per device.

```python
import math
import jax
import jax.numpy as jnp
from jax import lax

FEATS = 1024
ATOMS = 256
LAG = 500
BLOCK = 32
OUTB = 32
TRAJS = 16
HOMEB = 63
HOME = 2516


def draw_lengths(key, part):
    key = jax.random.fold_in(key, 11)
    key_order, key_split, key_chosen, key_tail = jax.random.split(key, 4)
    halfway = TRAJS // 2
    order = jax.random.permutation(key_order, TRAJS)
    split_at = jax.random.randint(key_split, (halfway,), 1, 2 * OUTB, dtype=jnp.int32)
    chosen = jax.random.randint(key_chosen, (), 0, halfway, dtype=jnp.int32)
    split_at = jnp.where(jnp.arange(halfway, dtype=jnp.int32) == chosen, 2 * OUTB - 1, split_at)
    counts_paired = jnp.stack([split_at, 2 * OUTB - split_at], axis=1).reshape(TRAJS)
    tails = jax.random.randint(key_tail, (TRAJS,), 1, BLOCK + 1, dtype=jnp.int32)
    tails = jnp.where(jnp.arange(TRAJS, dtype=jnp.int32) == 2 * chosen, BLOCK, tails)
    live = jnp.zeros((TRAJS,), jnp.int32).at[order].set(counts_paired)
    tail_rows = jnp.zeros((TRAJS,), jnp.int32).at[order].set(tails)
    return (LAG + (live - 1) * BLOCK + tail_rows).astype(jnp.int32)


def draw_atom_pairs(key, part):
    key = jax.random.fold_in(key, 12)
    key_first, key_step = jax.random.split(key, 2)
    first_atom = jax.random.randint(key_first, (FEATS,), 0, ATOMS, dtype=jnp.int32)
    stepping = jax.random.randint(key_step, (FEATS,), 1, ATOMS, dtype=jnp.int32)
    second_atom = (first_atom + stepping) % ATOMS
    return jnp.stack([first_atom, second_atom], axis=0).astype(jnp.int32)


def collective_motion(key, amplitude):
    mode_count = 128
    mode_terms = 4
    key_period, key_phase, key_member, key_loading = jax.random.split(key, 4)
    periods = LAG * jnp.exp(jax.random.uniform(key_period, (mode_count,), jnp.float32, math.log(3.0), math.log(12.0)))
    phases = jax.random.uniform(key_phase, (TRAJS, mode_count), jnp.float32, -math.pi, math.pi)
    members = jax.random.randint(key_member, (mode_terms, 3, ATOMS), 0, mode_count, dtype=jnp.int32)
    loadings = amplitude * jax.random.normal(key_loading, (mode_terms, 3, ATOMS), jnp.float32)
    frame_time = jnp.arange(HOME, dtype=jnp.float32)[None, :, None, None]
    motion = jnp.zeros((TRAJS, HOME, 3, ATOMS), jnp.float32)
    for term_index in range(mode_terms):
        angular_rate = 2.0 * math.pi / jnp.take(periods, members[term_index])
        offset = jnp.take(phases, members[term_index], axis=1)
        motion = motion + loadings[term_index] * jnp.sin(frame_time * angular_rate + offset[:, None])
    return motion


def draw_coords(key, part):
    key = jax.random.fold_in(key, 13)
    key_rest, key_drift, key_noise, key_motion = jax.random.split(key, 4)
    rest_shape = 0.45 * jax.random.normal(key_rest, (1, 1, 3, ATOMS), jnp.float32)
    drift_term = 0.12 * jax.random.normal(key_drift, (TRAJS, 1, 3, ATOMS), jnp.float32)
    noise_term = 0.12 * jax.random.normal(key_noise, (TRAJS, HOME, 3, ATOMS), jnp.float32)
    motion = collective_motion(key_motion, 0.1)
    values = jnp.clip(rest_shape + drift_term + motion + noise_term, -4.0, 4.0)
    return values.reshape(TRAJS * HOME, 3, ATOMS).astype(jnp.bfloat16)


def setup_inputs(seed: int = 0, part: int = 0) -> dict:
    streams_of = jax.random.split(jax.random.key(seed), 4)
    part_keys = jax.random.split(jax.random.fold_in(streams_of[3], part), 4)
    coords = draw_coords(jax.random.fold_in(jax.random.fold_in(streams_of[3], part), 71), part)
    lengths = draw_lengths(jax.random.fold_in(jax.random.fold_in(streams_of[3], part), 71), part)
    atom_pairs = draw_atom_pairs(jax.random.fold_in(streams_of[3], 71), part)
    return {"coords": coords, "lengths": lengths, "atom_pairs": atom_pairs}


def contacts(frames, atom_pairs):
    first_atom = jnp.take(frames, atom_pairs[0], axis=2).astype(jnp.float32)
    second_atom = jnp.take(frames, atom_pairs[1], axis=2).astype(jnp.float32)
    separation = first_atom - second_atom
    distance = jnp.sqrt(lax.optimization_barrier(jnp.sum(separation * separation, axis=1)))
    return jax.nn.sigmoid(6.0 * (1.0 - distance)).astype(jnp.bfloat16)

def reference(coords, lengths, atom_pairs):
    members = lengths.shape[0]
    stacked = coords.reshape(members, HOME, 3, ATOMS)
    window = HOMEB * BLOCK

    def accumulate(running, inputs):
        frames, length = inputs
        features = contacts(frames, atom_pairs)
        live_rows = (jnp.arange(window, dtype=jnp.int32) < length - LAG).astype(jnp.bfloat16)[:, None]
        leading = features[:window] * live_rows
        lagged = features[LAG:LAG + window] * live_rows
        gram_zero, gram_lag, start_sum, end_sum = running
        gram_zero = gram_zero + jnp.dot(leading.T, leading, preferred_element_type=jnp.float32)
        gram_lag = gram_lag + jnp.dot(leading.T, lagged, preferred_element_type=jnp.float32)
        start_sum = start_sum + lax.optimization_barrier(jnp.sum(leading, axis=0, dtype=jnp.float32))
        end_sum = end_sum + lax.optimization_barrier(jnp.sum(lagged, axis=0, dtype=jnp.float32))
        return ((gram_zero, gram_lag, start_sum, end_sum), None)
    initial = (jnp.zeros((FEATS, FEATS), jnp.float32), jnp.zeros((FEATS, FEATS), jnp.float32), jnp.zeros((FEATS,), jnp.float32), jnp.zeros((FEATS,), jnp.float32))
    running, _ = lax.scan(accumulate, initial, (stacked, lengths))
    gram_zero, gram_lag, start_sum, end_sum = running
    pair_total = jnp.sum(lengths - LAG).astype(jnp.float32)
    mean_lead = start_sum / pair_total
    mean_lag = end_sum / pair_total
    cov_zero = gram_zero / pair_total - jnp.outer(mean_lead, mean_lead)
    cov_lag = gram_lag / pair_total - jnp.outer(mean_lead, mean_lag)
    return (cov_zero, cov_lag)
```

```python
import functools

import jax
import jax.numpy as jnp
from jax import lax
from jax.experimental import pallas as pl
from jax.experimental.pallas import tpu as pltpu
from jax.sharding import PartitionSpec as P

LAG = 500
FRAME_TILE = 512
FEATURE_TILE = 256
DEPTH_UNIT = 256
SLOPE = 6.0 * 1.4426950408889634
LEVELS = 32752.0
SLACK = 2e-5
FLOOR = 1e-36
VMEM = 52 * 1024 * 1024


def round_up(value, unit):
    return -(-value // unit) * unit


def contacts_kernel(pairs_count, pairs_ref, coords_ref, features_ref, stats_ref, table_ref, *, home):
    step = pl.program_id(0)
    atoms, feats = table_ref.shape
    tile = features_ref.shape[0]

    @pl.when(step == 0)
    def _():
        atom_ids = lax.broadcasted_iota(jnp.int32, (atoms, feats), 0)
        first_hit = (atom_ids == pairs_ref[0:1, :]).astype(jnp.float32)
        second_hit = (atom_ids == pairs_ref[1:2, :]).astype(jnp.float32)
        table_ref[...] = (first_hit - second_hit).astype(jnp.bfloat16)
        stats_ref[...] = jnp.zeros_like(stats_ref)

    live = pairs_count[0]
    frame = step * tile + lax.broadcasted_iota(jnp.int32, (tile, 1), 0)
    lead_rows = (frame < live).astype(jnp.float32)
    lag_rows = ((frame >= LAG) & (frame < live + LAG)).astype(jnp.float32)
    for start in range(0, feats, FEATURE_TILE):
        columns = slice(start, start + FEATURE_TILE)
        weights = table_ref[:, columns]
        squared = None
        for axis in range(3):
            separation = jnp.dot(coords_ref[axis], weights, preferred_element_type=jnp.float32)
            square = separation * separation
            squared = square if squared is None else squared + square
        squared = jnp.maximum(squared, 1e-30)
        distance = squared * lax.rsqrt(squared)
        value = 1.0 / (1.0 + jnp.exp2(distance * SLOPE - SLOPE))
        value = jnp.where(frame < home, value, 0.0).astype(jnp.bfloat16)
        features_ref[:, columns] = value
        value = value.astype(jnp.float32)
        lead = value * lead_rows
        lag = value * lag_rows
        stats_ref[0:1, columns] += jnp.sum(lead, axis=0, keepdims=True)
        stats_ref[1:2, columns] += jnp.sum(lag, axis=0, keepdims=True)
        stats_ref[2:3, columns] += jnp.sum(lead * value, axis=0, keepdims=True)
        stats_ref[3:4, columns] += jnp.sum(lag * value, axis=0, keepdims=True)

    @pl.when(step == pl.num_programs(0) - 1)
    def _():
        totals = stats_ref[0:2, :]
        squares = stats_ref[2:4, :]
        spread = squares - totals * totals / live.astype(jnp.float32)
        stats_ref[2:4, :] = jnp.maximum(spread, 0.0) + (SLACK * squares + FLOOR)


def contact_features(coords, atom_pairs, live, rows):
    home, atoms = coords.shape[1], coords.shape[2]
    feats = atom_pairs.shape[1]
    return pl.pallas_call(
        functools.partial(contacts_kernel, home=home),
        grid=(rows // FRAME_TILE,),
        in_specs=[
            pl.BlockSpec(memory_space=pltpu.SMEM),
            pl.BlockSpec((2, feats), lambda i: (0, 0)),
            pl.BlockSpec((3, FRAME_TILE, atoms), lambda i: (0, i, 0)),
        ],
        out_specs=[
            pl.BlockSpec((FRAME_TILE, feats), lambda i: (i, 0)),
            pl.BlockSpec((8, feats), lambda i: (0, 0)),
        ],
        out_shape=[
            jax.ShapeDtypeStruct((rows, feats), jnp.bfloat16),
            jax.ShapeDtypeStruct((8, feats), jnp.float32),
        ],
        scratch_shapes=[pltpu.VMEM((atoms, feats), jnp.bfloat16)],
        compiler_params=pltpu.CompilerParams(vmem_limit_bytes=VMEM),
        name="contact_features",
    )(live, atom_pairs, coords)


def gram_kernel(scalars, features_ref, stats_ref, kept_ref, sent_ref, lead_ref, right_ref, *, lagged):
    live, side = scalars[0], scalars[1]
    depth, feats = lead_ref.shape
    half = feats // 2
    frame = lax.broadcasted_iota(jnp.int32, (depth, 1), 0)
    lead_ref[...] = jnp.where(frame < live, features_ref[0:depth, :], 0.0).astype(jnp.bfloat16)
    if lagged:
        right_ref[...] = features_ref[LAG : LAG + depth, :]
    else:
        right_ref = lead_ref
    other = 1 if lagged else 0
    stats = stats_ref[...]
    inverse = lax.rsqrt(stats)
    count = live.astype(jnp.float32)
    left_total = jnp.transpose(stats)[:, 0:1]
    left_inverse = jnp.transpose(inverse)[:, 2:3] * LEVELS
    own = pl.ds(pl.multiple_of(side * half, half), half)
    peer = pl.ds(pl.multiple_of((1 - side) * half, half), half)
    own_total = stats_ref[other : other + 1, own] / count
    peer_total = stats_ref[other : other + 1, peer] / count
    peer_inverse = lax.rsqrt(stats_ref[2 + other : 3 + other, peer])
    for start in range(0, feats, FEATURE_TILE):
        rows = slice(start, start + FEATURE_TILE)
        left = lead_ref[:, rows]
        kept = lax.dot_general(
            left, right_ref[:, own], (((0,), (0,)), ((), ())), preferred_element_type=jnp.float32
        )
        kept_ref[rows, :] = kept - left_total[rows] * own_total
        sent = lax.dot_general(
            left, right_ref[:, peer], (((0,), (0,)), ((), ())), preferred_element_type=jnp.float32
        )
        sent = (sent - left_total[rows] * peer_total) * (left_inverse[rows] * peer_inverse)
        sent_ref[rows, :] = jnp.round(sent).astype(jnp.int32).astype(jnp.int16)


def local_gram(features, stats, scalars, depth, lagged):
    rows, feats = features.shape
    whole = pl.BlockSpec(memory_space=pltpu.VMEM)
    return pl.pallas_call(
        functools.partial(gram_kernel, lagged=lagged),
        in_specs=[pl.BlockSpec(memory_space=pltpu.SMEM), whole, whole],
        out_specs=[whole, whole],
        out_shape=[
            jax.ShapeDtypeStruct((feats, feats // 2), jnp.float32),
            jax.ShapeDtypeStruct((feats, feats // 2), jnp.int16),
        ],
        scratch_shapes=[
            pltpu.VMEM((depth, feats), jnp.bfloat16),
            pltpu.VMEM((depth, feats) if lagged else (16, 128), jnp.bfloat16),
        ],
        compiler_params=pltpu.CompilerParams(vmem_limit_bytes=VMEM),
        name="gram_lag" if lagged else "gram_zero",
    )(scalars, features, stats)


def quantize(values, row_spread, column_spread):
    scale = (lax.rsqrt(row_spread) * LEVELS)[..., None] * lax.rsqrt(column_spread)
    return jnp.round(values * scale).astype(jnp.int16)


def restore(values, row_spread, column_spread):
    scale = (jnp.sqrt(row_spread) * (1.0 / LEVELS))[..., None] * jnp.sqrt(column_spread)
    return values.astype(jnp.float32) * scale


def exclusive(size, distance):
    return [(i, i ^ distance) for i in range(size)]


def local(coords, lengths, atom_pairs):
    members = lengths.shape[0]
    feats = atom_pairs.shape[1]
    half = feats // 2
    dp = lax.axis_size("dp")
    far = dp // 2
    block = feats // dp
    home = coords.shape[0]
    depth = round_up(home - LAG, DEPTH_UNIT)
    rows = round_up(max(home, depth + LAG), FRAME_TILE)
    dp_index = lax.axis_index("dp")
    side = lax.axis_index("tile")
    place = dp_index * 2 + side
    near_index = dp_index % 2
    far_index = dp_index // 2
    live = (lengths - LAG).astype(jnp.int32)
    own_live = lax.dynamic_slice_in_dim(live, place, 1)
    scalars = jnp.concatenate([own_live, side[None].astype(jnp.int32)])

    features, stats = contact_features(
        jnp.transpose(coords, (1, 0, 2)), atom_pairs, own_live, rows
    )
    kept_zero, sent_zero = local_gram(features, stats, scalars, depth, False)
    kept_lag, sent_lag = local_gram(features, stats, scalars, depth, True)

    stats = stats[0:4]
    peer_stats = lax.ppermute(stats, "tile", exclusive(2, 1))
    chip_sums = jnp.concatenate([stats[0:2], peer_stats[0:2]], axis=0)
    chip_spread = stats[2:4] + peer_stats[2:4]
    chip = jnp.concatenate([chip_sums, chip_spread], axis=0)
    near_chip = lax.ppermute(chip, "dp", exclusive(dp, 1))
    pair_spread = chip_spread + near_chip[4:6]
    gathered = jnp.concatenate([chip_sums, near_chip[0:4], pair_spread], axis=0)[None]
    distance = 1
    while distance < far:
        other = lax.ppermute(gathered, "dp", exclusive(dp, 2 * distance))
        gathered = jnp.concatenate([gathered, other], axis=0)
        distance *= 2

    def own_columns(vector):
        return lax.dynamic_slice_in_dim(vector, side * half, half, axis=-1)

    def reduce_over_group(kept, sent, which):
        came = lax.ppermute(sent, "tile", exclusive(2, 1))
        total = kept + restore(came, peer_stats[2], own_columns(peer_stats[2 + which]))
        total = total.reshape(far, 2, block, half)
        row_spread = chip_spread[0].reshape(far, 2, block)
        near_spread = near_chip[4].reshape(far, 2, block)
        to_near = lax.dynamic_index_in_dim(total, 1 - near_index, 1, keepdims=False)
        to_near = quantize(
            to_near,
            lax.dynamic_index_in_dim(row_spread, 1 - near_index, 1, keepdims=False),
            own_columns(chip_spread[which]),
        )
        came = lax.ppermute(to_near, "dp", exclusive(dp, 1))
        total = lax.dynamic_index_in_dim(total, near_index, 1, keepdims=False) + restore(
            came,
            lax.dynamic_index_in_dim(near_spread, near_index, 1, keepdims=False),
            own_columns(near_chip[4 + which]),
        )
        row_spread = pair_spread[0].reshape(far, 2, block)
        result = lax.dynamic_index_in_dim(total, far_index, 0, keepdims=False)
        for step in range(1, far):
            target = far_index ^ step
            to_far = quantize(
                lax.dynamic_index_in_dim(total, target, 0, keepdims=False),
                row_spread[target, near_index],
                own_columns(pair_spread[which]),
            )
            came = lax.ppermute(to_far, "dp", exclusive(dp, 2 * step))
            spread = gathered[step, 8].reshape(dp, block)[dp_index]
            result = result + restore(came, spread, own_columns(gathered[step, 8 + which]))
        return result

    within_zero = reduce_over_group(kept_zero, sent_zero, 0)
    within_lag = reduce_over_group(kept_lag, sent_lag, 1)

    pair_total = jnp.sum(live).astype(jnp.float32)
    order = place ^ jnp.arange(members, dtype=jnp.int32)
    weight = jnp.take(live, order).astype(jnp.float32)
    sums = gathered[:, 0:8].reshape(members, 2, feats)
    shift = sums / weight[:, None, None] - jnp.sum(sums, axis=0) / pair_total
    lead_shift = lax.dynamic_slice_in_dim(shift[:, 0], dp_index * block, block, axis=1)
    lead_shift = lead_shift * weight[:, None]
    columns = own_columns(shift)

    def between(right):
        return lax.dot_general(
            lead_shift, right, (((0,), (0,)), ((), ())), precision=lax.Precision.HIGHEST
        )

    cov_zero = (within_zero + between(columns[:, 0])) / pair_total
    cov_lag = (within_lag + between(columns[:, 1])) / pair_total
    return (cov_zero, cov_lag)


def solution(mesh):
    placed = (P(("groups", "dp", "tile"), None, None), P("groups"), P())
    return jax.shard_map(
        local,
        mesh=mesh,
        in_specs=placed,
        out_specs=(P(("groups", "dp"), "tile"), P(("groups", "dp"), "tile")),
        check_vma=False,
    )
```

```python
import functools

import jax
import jax.numpy as jnp
from jax import lax
from jax.experimental import pallas as pl
from jax.experimental.pallas import tpu as pltpu
from jax.sharding import PartitionSpec as P

LAG = 500
FRAME_TILE = 512
FEATURE_TILE = 256
DEPTH_UNIT = 256
SLOPE = 6.0 * 1.4426950408889634
LEVELS = 32752.0
SLACK = 2e-5
FLOOR = 1e-36
VMEM = 24 * 1024 * 1024
WHOLE = pl.BlockSpec(memory_space=pltpu.VMEM)
SCALARS = pl.BlockSpec(memory_space=pltpu.SMEM)


def round_up(value, unit):
    return -(-value // unit) * unit


def own_place():
    return lax.axis_index("dp") * lax.axis_size("tile") + lax.axis_index("tile")


def params():
    return pltpu.CompilerParams(vmem_limit_bytes=VMEM)


def cost(depth, feats):
    return pl.CostEstimate(flops=depth * feats * feats, bytes_accessed=2 * depth * feats, transcendentals=0)


def shape(dims, dtype=jnp.float32):
    return jax.ShapeDtypeStruct(dims, dtype)


def to_levels(values):
    return jnp.round(values).astype(jnp.int32).astype(jnp.int16)


def from_levels(values):
    return values.astype(jnp.int32).astype(jnp.float32)


def side_columns(half, own):
    side = lax.axis_index("tile")
    return pl.ds(pl.multiple_of((side if own else 1 - side) * half, half), half)


def load_right(features_ref, right_ref, own, lagged):
    depth, half = right_ref.shape
    first = LAG if lagged else 0
    right_ref[...] = features_ref[first : first + depth, side_columns(half, own)]


def gram_rows(features_ref, right_ref, start, live):
    depth = right_ref.shape[0]
    alive = lax.broadcasted_iota(jnp.int32, (depth, 1), 0) < live
    left = jnp.where(alive, features_ref[0:depth, start : start + FEATURE_TILE], 0.0)
    return lax.dot_general(
        left.astype(jnp.bfloat16),
        right_ref[...],
        (((0,), (0,)), ((), ())),
        preferred_element_type=jnp.float32,
    )


def sent_gram(features_ref, stats_ref, sent_ref, right_ref, live, lagged):
    feats, half = sent_ref.shape
    load_right(features_ref, right_ref, False, lagged)
    columns = side_columns(half, False)
    right = 1 if lagged else 0
    left_stats = jnp.transpose(stats_ref[...])
    right_mean = stats_ref[right : right + 1, columns] / live.astype(jnp.float32)
    right_inverse = lax.rsqrt(stats_ref[2:3, columns])
    for start in range(0, feats, FEATURE_TILE):
        rows = slice(start, start + FEATURE_TILE)
        gram = gram_rows(features_ref, right_ref, start, live)
        gram = gram - left_stats[rows, 0:1] * right_mean
        scale = (lax.rsqrt(left_stats[rows, 2:3]) * LEVELS) * right_inverse
        sent_ref[rows, :] = to_levels(gram * scale)


def contacts_kernel(lengths_ref, pairs_ref, coords_ref, features_ref, stats_ref, table_ref):
    step = pl.program_id(0)
    atoms, feats = table_ref.shape
    tile = coords_ref.shape[1]

    @pl.when(step == 0)
    def _():
        atom_ids = lax.broadcasted_iota(jnp.int32, (atoms, feats), 0)
        first_hit = (atom_ids == pairs_ref[0:1, :]).astype(jnp.float32)
        second_hit = (atom_ids == pairs_ref[1:2, :]).astype(jnp.float32)
        table_ref[...] = (first_hit - second_hit).astype(jnp.bfloat16)
        stats_ref[...] = jnp.zeros_like(stats_ref)

    live = lengths_ref[own_place()] - LAG
    frame = step * tile + lax.broadcasted_iota(jnp.int32, (tile, 1), 0)
    used = (frame < live) | ((frame >= LAG) & (frame < live + LAG))
    row = lax.broadcasted_iota(jnp.int32, (8, tile), 0)
    column = step * tile + lax.broadcasted_iota(jnp.int32, (8, tile), 1)
    leads = column < live
    lags = (column >= LAG) & (column < live + LAG)
    masks = ((row == 0) & leads) | ((row == 1) & lags) | ((row == 2) & (leads | lags))
    masks = masks.astype(jnp.float32).astype(jnp.bfloat16)
    target = pl.ds(pl.multiple_of(step * tile, tile), tile)
    for start in range(0, feats, FEATURE_TILE):
        columns = slice(start, start + FEATURE_TILE)
        weights = table_ref[:, columns]
        squared = None
        for axis in range(3):
            separation = jnp.dot(coords_ref[axis], weights, preferred_element_type=jnp.float32)
            square = separation * separation
            squared = square if squared is None else squared + square
        squared = jnp.maximum(squared, 1e-30)
        distance = squared * lax.rsqrt(squared)
        value = pl.reciprocal(1.0 + jnp.exp2(distance * SLOPE - SLOPE), approx=True)
        value = jnp.where(used, value, 0.0).astype(jnp.bfloat16)
        features_ref[target, columns] = value
        stats_ref[:, columns] += jnp.dot(masks, value, preferred_element_type=jnp.float32)
        value = value.astype(jnp.float32)
        stats_ref[3:4, columns] += jnp.sum(value * value, axis=0, keepdims=True)

    @pl.when(step == pl.num_programs(0) - 1)
    def _():
        count = live + jnp.minimum(live, LAG)
        total = stats_ref[2:3, :]
        squares = stats_ref[3:4, :]
        spread = squares - total * total / count.astype(jnp.float32)
        stats_ref[2:3, :] = jnp.maximum(spread, 0.0) + (SLACK * squares + FLOOR)


def contacts_call(coords, lengths, atom_pairs, rows):
    atoms = coords.shape[2]
    feats = atom_pairs.shape[1]
    return pl.pallas_call(
        contacts_kernel,
        grid=(rows // FRAME_TILE,),
        in_specs=[
            SCALARS,
            pl.BlockSpec((2, feats), lambda i: (0, 0)),
            pl.BlockSpec((3, FRAME_TILE, atoms), lambda i: (0, i, 0)),
        ],
        out_specs=[WHOLE, WHOLE],
        out_shape=[shape((rows, feats), jnp.bfloat16), shape((8, feats))],
        scratch_shapes=[pltpu.VMEM((atoms, feats), jnp.bfloat16)],
        compiler_params=params(),
        name="contacts",
    )(lengths, atom_pairs, coords)


def sent_lag_kernel(lengths_ref, features_ref, stats_ref, sent_ref, right_ref):
    live = lengths_ref[own_place()] - LAG
    sent_gram(features_ref, stats_ref, sent_ref, right_ref, live, True)


def sent_zero_kernel(lengths_ref, features_ref, stats_ref, peer_ref, sent_ref, chip_ref, right_ref):
    live = lengths_ref[own_place()] - LAG
    chip_ref[0:2, :] = stats_ref[0:2, :]
    chip_ref[2:4, :] = peer_ref[0:2, :]
    chip_ref[4:8, :] = jnp.broadcast_to(stats_ref[2:3, :] + peer_ref[2:3, :], (4, stats_ref.shape[1]))
    sent_gram(features_ref, stats_ref, sent_ref, right_ref, live, False)


def sent_call(lengths, features, stats, peer, depth):
    feats = features.shape[1]
    sent = shape((feats, feats // 2), jnp.int16)
    operands = [lengths, features, stats] + ([] if peer is None else [peer])
    return pl.pallas_call(
        sent_lag_kernel if peer is None else sent_zero_kernel,
        in_specs=[SCALARS] + [WHOLE] * (len(operands) - 1),
        out_specs=WHOLE if peer is None else [WHOLE, WHOLE],
        out_shape=sent if peer is None else [sent, shape((8, feats))],
        scratch_shapes=[pltpu.VMEM((depth, feats // 2), jnp.bfloat16)],
        compiler_params=params(),
        cost_estimate=cost(depth, feats),
        name="sent_lag" if peer is None else "sent_zero",
    )(*operands)


def near_kernel(lengths_ref, features_ref, stats_ref, peer_ref, came_ref, *refs, lagged, block):
    if lagged:
        keep_ref, sent_ref, right_ref = refs
    else:
        chip_ref, near_ref, _, keep_ref, sent_ref, pair_ref, right_ref = refs
        pair_ref[0, 0:4, :] = chip_ref[0:4, :]
        pair_ref[0, 4:8, :] = near_ref[0:4, :]
        pair_ref[0, 8:16, :] = jnp.broadcast_to(chip_ref[4:5, :] + near_ref[4:5, :], (8, chip_ref.shape[1]))
    live = lengths_ref[own_place()] - LAG
    near = lax.axis_index("dp") % 2
    feats, half = came_ref.shape
    load_right(features_ref, right_ref, True, lagged)
    columns = side_columns(half, True)
    right = 1 if lagged else 0
    chip_spread = stats_ref[2:3, :] + peer_ref[2:3, :]
    left = jnp.concatenate([stats_ref[0:1, :], peer_ref[2:3, :], chip_spread, chip_spread], axis=0)
    left = jnp.transpose(jnp.concatenate([left, left], axis=0))
    right_mean = stats_ref[right : right + 1, columns] / live.astype(jnp.float32)
    came_right = jnp.sqrt(peer_ref[2:3, columns])
    sent_right = lax.rsqrt(stats_ref[2:3, columns] + peer_ref[2:3, columns])
    for start in range(0, feats, FEATURE_TILE):
        rows = slice(start, start + FEATURE_TILE)
        gram = gram_rows(features_ref, right_ref, start, live)
        gram = gram - left[rows, 0:1] * right_mean
        scale = (jnp.sqrt(left[rows, 1:2]) * (1.0 / LEVELS)) * came_right
        gram = gram + from_levels(came_ref[rows, :]) * scale
        spread = left[rows, 2:3]
        for first in range(0, FEATURE_TILE, 2 * block):
            even, odd = slice(first, first + block), slice(first + block, first + 2 * block)
            place = (start + first) // 2
            target = slice(place, place + block)
            keep_ref[target, :] = jnp.where(near == 0, gram[even], gram[odd])
            other = jnp.where(near == 0, gram[odd], gram[even])
            other_spread = jnp.where(near == 0, spread[odd], spread[even])
            scale = (lax.rsqrt(other_spread) * LEVELS) * sent_right
            sent_ref[target, :] = to_levels(other * scale)


def near_call(lengths, features, stats, peer, came, after, depth, block, lagged):
    feats, half = came.shape
    outs = [shape((half, half)), shape((half, half), jnp.int16)]
    specs = [SCALARS] + [WHOLE] * 4
    if not lagged:
        outs.append(shape((1, 16, feats)))
        specs += [WHOLE, WHOLE, pl.BlockSpec(memory_space=pl.ANY)]
    return pl.pallas_call(
        functools.partial(near_kernel, lagged=lagged, block=block),
        in_specs=specs,
        out_specs=[WHOLE] * len(outs),
        out_shape=outs,
        scratch_shapes=[pltpu.VMEM((depth, half), jnp.bfloat16)],
        compiler_params=params(),
        cost_estimate=cost(depth, feats),
        name="kept_lag" if lagged else "kept_zero",
    )(lengths, features, stats, peer, came, *after)


def far_kernel(keep_ref, came_ref, chip_ref, near_ref, *refs, block):
    kept_ref, sent_refs = refs[0], refs[1:-2]
    total_ref, level_ref = refs[-2], refs[-1]
    place = lax.axis_index("dp")
    near, far = place % 2, place // 2
    half = came_ref.shape[0]
    feats = chip_ref.shape[1]
    columns = side_columns(half, True)
    pair = chip_ref[4:5, :] + near_ref[4:5, :]
    left = jnp.concatenate([near_ref[4:5, :], pair] * 4, axis=0)
    left = jnp.transpose(left)
    came_right = jnp.sqrt(near_ref[4:5, columns])
    sent_right = lax.rsqrt(chip_ref[4:5, columns] + near_ref[4:5, columns])
    for index in range(half // block):
        rows = slice(index * block, (index + 1) * block)
        even = left[2 * index * block : (2 * index + 1) * block]
        odd = left[(2 * index + 1) * block : (2 * index + 2) * block]
        mine = jnp.where(near == 0, even, odd)
        scale = (jnp.sqrt(mine[:, 0:1]) * (1.0 / LEVELS)) * came_right
        total = keep_ref[rows, :] + from_levels(came_ref[rows, :]) * scale
        total_ref[index] = total
        scale = (lax.rsqrt(mine[:, 1:2]) * LEVELS) * sent_right
        level_ref[index] = to_levels(total * scale)
    kept_ref[...] = total_ref[far]
    for step, sent_ref in enumerate(sent_refs):
        sent_ref[...] = level_ref[far ^ (step + 1)]


def far_call(keep, came, chip, near, block, name):
    half = came.shape[0]
    far = half // block
    return pl.pallas_call(
        functools.partial(far_kernel, block=block),
        in_specs=[WHOLE] * 4,
        out_specs=[WHOLE] * far,
        out_shape=[shape((block, half))] + [shape((block, half), jnp.int16)] * (far - 1),
        scratch_shapes=[
            pltpu.VMEM((far, block, half), jnp.float32),
            pltpu.VMEM((far, block, half), jnp.int16),
        ],
        compiler_params=params(),
        name=name,
    )(keep, came, chip, near)


def gathered_total(kept_ref, came_refs, left_ref, stats_ref, columns):
    total = kept_ref[...]
    width = stats_ref.shape[1]
    for index, came_ref in enumerate(came_refs):
        spread = width * (index + 1) + 8
        scale = jnp.sqrt(left_ref[:, spread : spread + 1]) * (1.0 / LEVELS)
        scale = scale * jnp.sqrt(stats_ref[index + 1, 8:9, columns])
        total = total + from_levels(came_ref[...]) * scale
    return total


def finish_lag_kernel(lengths_ref, left_ref, stats_ref, kept_ref, *refs):
    came_refs, out_ref, zero_ref = refs[:-2], refs[-2], refs[-1]
    groups, width = stats_ref.shape[0:2]
    members = 4 * groups
    columns = side_columns(kept_ref.shape[1], True)
    place = own_place()
    pair_total = lax.fori_loop(0, members, lambda i, t: t + lengths_ref[i] - LAG, 0)
    pair_total = pair_total.astype(jnp.float32)
    lead_mean = lead_row = lag_row = 0.0
    for group in range(groups):
        for member in range(4):
            first = 2 * member
            lead_mean += left_ref[:, width * group + first : width * group + first + 1]
            lead_row += stats_ref[group, first : first + 1, columns]
            lag_row += stats_ref[group, first + 1 : first + 2, columns]
    lead_mean, lead_row, lag_row = (v / pair_total for v in (lead_mean, lead_row, lag_row))
    lag = gathered_total(kept_ref, came_refs, left_ref, stats_ref, columns)
    zero = jnp.zeros_like(lag)
    for group in range(groups):
        for member in range(4):
            first = 2 * member
            weight = (lengths_ref[place ^ (4 * group + member)] - LAG).astype(jnp.float32)
            lead = left_ref[:, width * group + first : width * group + first + 1]
            lead = lead - lead_mean * weight
            zero = zero + lead * (stats_ref[group, first : first + 1, columns] / weight - lead_row)
            lag = lag + lead * (stats_ref[group, first + 1 : first + 2, columns] / weight - lag_row)
    out_ref[...] = lag / pair_total
    zero_ref[...] = zero


def finish_lag(lengths, left, stats, kept, came):
    return pl.pallas_call(
        finish_lag_kernel,
        in_specs=[SCALARS] + [WHOLE] * (3 + len(came)),
        out_specs=[WHOLE, WHOLE],
        out_shape=[shape(kept.shape), shape(kept.shape)],
        compiler_params=params(),
        name="finish_lag",
    )(lengths, left, stats, kept, *came)


def finish_zero_kernel(lengths_ref, left_ref, stats_ref, between_ref, kept_ref, *refs):
    came_refs, out_ref = refs[:-1], refs[-1]
    members = 4 * stats_ref.shape[0]
    columns = side_columns(kept_ref.shape[1], True)
    pair_total = lax.fori_loop(0, members, lambda i, t: t + lengths_ref[i] - LAG, 0)
    zero = gathered_total(kept_ref, came_refs, left_ref, stats_ref, columns)
    out_ref[...] = (zero + between_ref[...]) / pair_total.astype(jnp.float32)


def finish_zero(lengths, left, stats, between, kept, came):
    return pl.pallas_call(
        finish_zero_kernel,
        in_specs=[SCALARS] + [WHOLE] * (4 + len(came)),
        out_specs=WHOLE,
        out_shape=shape(kept.shape),
        compiler_params=params(),
        name="finish_zero",
    )(lengths, left, stats, between, kept, *came)


def exclusive(size, distance):
    return [(i, i ^ distance) for i in range(size)]


def local(coords, lengths, atom_pairs):
    feats = atom_pairs.shape[1]
    dp = lax.axis_size("dp")
    far = dp // 2
    block = feats // dp
    home = coords.shape[0]
    depth = round_up(home - LAG, DEPTH_UNIT)
    rows = round_up(max(home, depth + LAG), FRAME_TILE)

    def swap(array, axis, distance):
        return lax.ppermute(array, axis, exclusive(lax.axis_size(axis), distance))

    coords = pltpu.with_memory_space_constraint(jnp.transpose(coords, (1, 0, 2)), pltpu.HBM)
    features, stats = contacts_call(coords, lengths, atom_pairs, rows)
    peer = swap(stats, "tile", 1)
    sent_lag = sent_call(lengths, features, stats, None, depth)
    came_lag = swap(sent_lag, "tile", 1)
    sent_zero, chip = sent_call(lengths, features, stats, peer, depth)
    near = swap(chip, "dp", 1)
    came_zero = swap(sent_zero, "tile", 1)
    keep_lag, sent_lag = near_call(
        lengths, features, stats, peer, came_lag, [], depth, block, True
    )
    came_lag = swap(sent_lag, "dp", 1)
    keep_zero, sent_zero, gathered = near_call(
        lengths, features, stats, peer, came_zero, [chip, near, sent_lag], depth, block, False
    )
    came_zero = swap(sent_zero, "dp", 1)

    distance = 1
    while distance < far:
        other = swap(gathered, "dp", 2 * distance)
        gathered = jnp.concatenate([gathered, other], axis=0)
        distance *= 2
    left = lax.dynamic_slice_in_dim(
        gathered.reshape(-1, feats), lax.axis_index("dp") * block, block, axis=1
    ).T

    kept_lag, *sent_lag = far_call(keep_lag, came_lag, chip, near, block, "far_lag")
    came_lag = [swap(s, "dp", 2 * (i + 1)) for i, s in enumerate(sent_lag)]
    kept_zero, *sent_zero = far_call(keep_zero, came_zero, chip, near, block, "far_zero")
    came_zero = [swap(s, "dp", 2 * (i + 1)) for i, s in enumerate(sent_zero)]
    cov_lag, between = finish_lag(lengths, left, gathered, kept_lag, came_lag)
    cov_zero = finish_zero(lengths, left, gathered, between, kept_zero, came_zero)
    return (cov_zero, cov_lag)


def solution(mesh):
    placed = (P(("groups", "dp", "tile"), None, None), P("groups"), P())
    return jax.shard_map(
        local,
        mesh=mesh,
        in_specs=placed,
        out_specs=(P(("groups", "dp"), "tile"), P(("groups", "dp"), "tile")),
        check_vma=False,
    )
```

```python
import functools

import jax
import jax.numpy as jnp
from jax import lax
from jax.experimental import pallas as pl
from jax.experimental.pallas import tpu as pltpu
from jax.sharding import PartitionSpec as P

LAG = 500
FRAME_TILE = 512
FEATURE_TILE = 256
DEPTH_UNIT = 256
SLOPE = 6.0 * 1.4426950408889634
LEVELS = 32752.0
SLACK = 2e-5
FLOOR = 1e-36
LONG = 1 << 31
VMEM = 12 * 1024 * 1024
WHOLE = pl.BlockSpec(memory_space=pltpu.VMEM)
SCALARS = pl.BlockSpec(memory_space=pltpu.SMEM)


def round_up(value, unit):
    return -(-value // unit) * unit


def own_place():
    return lax.axis_index("dp") * lax.axis_size("tile") + lax.axis_index("tile")


def params():
    return pltpu.CompilerParams(vmem_limit_bytes=VMEM)


def shape(dims, dtype=jnp.float32):
    return jax.ShapeDtypeStruct(dims, dtype)


def to_levels(values):
    return jnp.round(values).astype(jnp.int32).astype(jnp.int16)


def from_levels(values):
    return values.astype(jnp.int32).astype(jnp.float32)


def side_columns(half, own):
    side = lax.axis_index("tile")
    return pl.ds(pl.multiple_of((side if own else 1 - side) * half, half), half)


def load_right(features_ref, right_ref, own, lagged):
    depth, half = right_ref.shape
    first = LAG if lagged else 0
    right_ref[...] = features_ref[first : first + depth, side_columns(half, own)]


def gram_rows(features_ref, right_ref, start, live):
    depth = right_ref.shape[0]
    alive = lax.broadcasted_iota(jnp.int32, (depth, 1), 0) < live
    left = jnp.where(alive, features_ref[0:depth, start : start + FEATURE_TILE], 0.0)
    return lax.dot_general(
        left.astype(jnp.bfloat16),
        right_ref[...],
        (((0,), (0,)), ((), ())),
        preferred_element_type=jnp.float32,
    )


def contacts_kernel(lengths_ref, pairs_ref, coords_ref, features_ref, stats_ref, table_ref):
    step = pl.program_id(0)
    atoms, feats = table_ref.shape
    tile = coords_ref.shape[1]

    @pl.when(step == 0)
    def _():
        atom_ids = lax.broadcasted_iota(jnp.int32, (atoms, feats), 0)
        first_hit = (atom_ids == pairs_ref[0:1, :]).astype(jnp.float32)
        second_hit = (atom_ids == pairs_ref[1:2, :]).astype(jnp.float32)
        table_ref[...] = (first_hit - second_hit).astype(jnp.bfloat16)
        stats_ref[...] = jnp.zeros_like(stats_ref)

    live = lengths_ref[own_place()] - LAG
    frame = step * tile + lax.broadcasted_iota(jnp.int32, (tile, 1), 0)
    used = (frame < live) | ((frame >= LAG) & (frame < live + LAG))
    leads = (step * tile + tile <= live).astype(jnp.float32)
    target = pl.ds(pl.multiple_of(step * tile, tile), tile)
    for start in range(0, feats, FEATURE_TILE):
        columns = slice(start, start + FEATURE_TILE)
        weights = table_ref[:, columns]
        squared = None
        for axis in range(3):
            separation = jnp.dot(coords_ref[axis], weights, preferred_element_type=jnp.float32)
            square = separation * separation
            squared = square if squared is None else squared + square
        squared = jnp.maximum(squared, 1e-30)
        distance = squared * lax.rsqrt(squared)
        value = pl.reciprocal(1.0 + jnp.exp2(distance * SLOPE - SLOPE), approx=True)
        value = jnp.where(used, value, 0.0).astype(jnp.bfloat16)
        features_ref[target, columns] = value
        value = value.astype(jnp.float32)
        total = jnp.sum(value, axis=0, keepdims=True)
        stats_ref[0:1, columns] += total * leads
        stats_ref[2:3, columns] += total
        stats_ref[3:4, columns] += jnp.sum(value * value, axis=0, keepdims=True)

    @pl.when((step * tile < live) & (step * tile + tile > live))
    def _():
        value = jnp.where(frame < live, features_ref[target, :], 0.0).astype(jnp.float32)
        stats_ref[0:1, :] += jnp.sum(value, axis=0, keepdims=True)

    @pl.when(step == 0)
    def _():
        value = features_ref[0:LAG, :].astype(jnp.float32)
        stats_ref[1:2, :] = -jnp.sum(value, axis=0, keepdims=True)

    @pl.when(step == pl.num_programs(0) - 1)
    def _():
        count = live + jnp.minimum(live, LAG)
        total = stats_ref[2:3, :]
        squares = stats_ref[3:4, :]
        stats_ref[1:2, :] += total
        spread = squares - total * total / count.astype(jnp.float32)
        stats_ref[2:3, :] = jnp.maximum(spread, 0.0) + (SLACK * squares + FLOOR)


def contacts_call(coords, lengths, atom_pairs, rows):
    atoms = coords.shape[2]
    feats = atom_pairs.shape[1]
    return pl.pallas_call(
        contacts_kernel,
        grid=(rows // FRAME_TILE,),
        in_specs=[
            SCALARS,
            pl.BlockSpec((2, feats), lambda i: (0, 0)),
            pl.BlockSpec((3, FRAME_TILE, atoms), lambda i: (0, i, 0)),
        ],
        out_specs=[WHOLE, WHOLE],
        out_shape=[shape((rows, feats), jnp.bfloat16), shape((8, feats))],
        scratch_shapes=[pltpu.VMEM((atoms, feats), jnp.bfloat16)],
        compiler_params=params(),
        name="contacts",
    )(lengths, atom_pairs, coords)


def gram_half(features_ref, stats_ref, out_refs, right_ref, live, kept, lagged):
    part, half = out_refs[0].shape
    feats = 2 * half
    load_right(features_ref, right_ref, kept, lagged)
    columns = side_columns(half, kept)
    right = 1 if lagged else 0
    left_stats = jnp.transpose(stats_ref[...])
    right_mean = stats_ref[right : right + 1, columns] / live.astype(jnp.float32)
    right_inverse = lax.rsqrt(stats_ref[2:3, columns])
    for start in range(0, feats, FEATURE_TILE):
        rows = slice(start, start + FEATURE_TILE)
        gram = gram_rows(features_ref, right_ref, start, live)
        gram = gram - left_stats[rows, 0:1] * right_mean
        if not kept:
            scale = (lax.rsqrt(left_stats[rows, 2:3]) * LEVELS) * right_inverse
            gram = to_levels(gram * scale)
        first = start % part
        out_refs[start // part][first : first + FEATURE_TILE, :] = gram


def sent_lag_kernel(lengths_ref, features_ref, stats_ref, sent_ref, right_ref):
    live = lengths_ref[own_place()] - LAG
    gram_half(features_ref, stats_ref, [sent_ref], right_ref, live, False, True)


def kept_lag_kernel(lengths_ref, features_ref, stats_ref, _, kept_ref, right_ref):
    live = lengths_ref[own_place()] - LAG
    gram_half(features_ref, stats_ref, [kept_ref], right_ref, live, True, True)


def sent_zero_kernel(lengths_ref, features_ref, stats_ref, peer_ref, sent_ref, chip_ref, right_ref):
    live = lengths_ref[own_place()] - LAG
    feats = stats_ref.shape[1]
    chip_ref[0:2, :] = stats_ref[0:2, :]
    chip_ref[2:4, :] = peer_ref[0:2, :]
    chip_ref[4:8, :] = jnp.broadcast_to(stats_ref[2:3, :] + peer_ref[2:3, :], (4, feats))
    gram_half(features_ref, stats_ref, [sent_ref], right_ref, live, False, False)


def kept_zero_kernel(
    lengths_ref, features_ref, stats_ref, chip_ref, near_ref, _, kept_ref, pair_ref, right_ref
):
    live = lengths_ref[own_place()] - LAG
    feats = stats_ref.shape[1]
    pair_ref[0:4, :] = chip_ref[0:4, :]
    pair_ref[4:8, :] = near_ref[0:4, :]
    pair_ref[8:16, :] = jnp.broadcast_to(chip_ref[4:5, :] + near_ref[4:5, :], (8, feats))
    gram_half(features_ref, stats_ref, [kept_ref], right_ref, live, True, False)


def gram_call(body, operands, after, outs, depth, estimate):
    feats = operands[1].shape[1]
    return pl.pallas_call(
        body,
        in_specs=[SCALARS]
        + [WHOLE] * (len(operands) - 1)
        + [pl.BlockSpec(memory_space=pl.ANY)] * len(after),
        out_specs=[WHOLE] * len(outs),
        out_shape=outs,
        scratch_shapes=[pltpu.VMEM((depth, feats // 2), jnp.bfloat16)],
        compiler_params=params(),
        cost_estimate=pl.CostEstimate(flops=estimate, bytes_accessed=estimate // 1024, transcendentals=0),
        name=body.__name__.removesuffix("_kernel"),
    )(*operands, *after)


def near_kernel(kept_ref, stats_ref, peer_ref, *refs, block):
    came_refs, keep_ref, sent_ref = refs[:-2], refs[-2], refs[-1]
    near = lax.axis_index("dp") % 2
    part = came_refs[0].shape[0]
    feats, half = kept_ref.shape
    columns = side_columns(half, True)
    chip_spread = stats_ref[2:3, :] + peer_ref[2:3, :]
    left = jnp.concatenate([peer_ref[2:3, :], chip_spread] * 4, axis=0)
    left = jnp.transpose(left)
    came_right = jnp.sqrt(peer_ref[2:3, columns])
    sent_right = lax.rsqrt(stats_ref[2:3, columns] + peer_ref[2:3, columns])
    for start in range(0, feats, 2 * block):
        totals = []
        for rows in (slice(start, start + block), slice(start + block, start + 2 * block)):
            scale = (jnp.sqrt(left[rows, 0:1]) * (1.0 / LEVELS)) * came_right
            first = rows.start % part
            came = came_refs[rows.start // part][first : first + block, :]
            totals.append(kept_ref[rows, :] + from_levels(came) * scale)
        target = slice(start // 2, start // 2 + block)
        keep_ref[target, :] = jnp.where(near == 0, totals[0], totals[1])
        other = jnp.where(near == 0, totals[1], totals[0])
        even = left[start : start + block, 1:2]
        odd = left[start + block : start + 2 * block, 1:2]
        scale = (lax.rsqrt(jnp.where(near == 0, odd, even)) * LEVELS) * sent_right
        sent_ref[target, :] = to_levels(other * scale)


def near_call(kept, came, stats, peer, block, name):
    half = kept.shape[1]
    return pl.pallas_call(
        functools.partial(near_kernel, block=block),
        in_specs=[WHOLE] * (3 + len(came)),
        out_specs=[WHOLE, WHOLE],
        out_shape=[shape((half, half)), shape((half, half), jnp.int16)],
        compiler_params=params(),
        name=name,
    )(kept, stats, peer, *came)


def far_kernel(keep_ref, came_ref, chip_ref, near_ref, *refs, block):
    kept_ref, sent_refs = refs[0], refs[1:-2]
    total_ref, level_ref = refs[-2], refs[-1]
    place = lax.axis_index("dp")
    near, far = place % 2, place // 2
    half = came_ref.shape[0]
    feats = chip_ref.shape[1]
    columns = side_columns(half, True)
    pair = chip_ref[4:5, :] + near_ref[4:5, :]
    left = jnp.concatenate([near_ref[4:5, :], pair] * 4, axis=0)
    left = jnp.transpose(left)
    came_right = jnp.sqrt(near_ref[4:5, columns])
    sent_right = lax.rsqrt(chip_ref[4:5, columns] + near_ref[4:5, columns])
    for index in range(half // block):
        rows = slice(index * block, (index + 1) * block)
        even = left[2 * index * block : (2 * index + 1) * block]
        odd = left[(2 * index + 1) * block : (2 * index + 2) * block]
        mine = jnp.where(near == 0, even, odd)
        scale = (jnp.sqrt(mine[:, 0:1]) * (1.0 / LEVELS)) * came_right
        total = keep_ref[rows, :] + from_levels(came_ref[rows, :]) * scale
        total_ref[index] = total
        scale = (lax.rsqrt(mine[:, 1:2]) * LEVELS) * sent_right
        level_ref[index] = to_levels(total * scale)
    kept_ref[...] = total_ref[far]
    for step, sent_ref in enumerate(sent_refs):
        sent_ref[...] = level_ref[far ^ (step + 1)]


def far_call(keep, came, chip, near, block, name):
    half = came.shape[0]
    far = half // block
    return pl.pallas_call(
        functools.partial(far_kernel, block=block),
        in_specs=[WHOLE] * 4,
        out_specs=[WHOLE] * far,
        out_shape=[shape((block, half))] + [shape((block, half), jnp.int16)] * (far - 1),
        scratch_shapes=[
            pltpu.VMEM((far, block, half), jnp.float32),
            pltpu.VMEM((far, block, half), jnp.int16),
        ],
        compiler_params=params(),
        name=name,
    )(keep, came, chip, near)


def gathered_total(kept_ref, came_refs, left_ref, stats_refs, columns):
    total = kept_ref[...]
    for index, came_ref in enumerate(came_refs):
        spread = left_ref[:, 16 * index + 24 : 16 * index + 25]
        scale = jnp.sqrt(spread) * (1.0 / LEVELS)
        scale = scale * jnp.sqrt(stats_refs[index + 1][8:9, columns])
        total = total + from_levels(came_ref[...]) * scale
    return total


def pairs_of(lengths_ref, members):
    total = lax.fori_loop(0, members, lambda i, t: t + lengths_ref[i] - LAG, 0)
    return total.astype(jnp.float32)


def finish_lag_kernel(lengths_ref, left_ref, kept_ref, *refs):
    groups = len(refs) // 2
    stats_refs, came_refs, out_ref, zero_ref = refs[:groups], refs[groups:-2], refs[-2], refs[-1]
    columns = side_columns(kept_ref.shape[1], True)
    place = own_place()
    pair_total = pairs_of(lengths_ref, 4 * groups)
    members = [(group, member) for group in range(groups) for member in range(4)]
    lead_mean = lead_row = lag_row = 0.0
    for group, member in members:
        column = 16 * group + 2 * member
        lead_mean += left_ref[:, column : column + 1]
        lead_row += stats_refs[group][2 * member : 2 * member + 1, columns]
        lag_row += stats_refs[group][2 * member + 1 : 2 * member + 2, columns]
    lead_mean, lead_row, lag_row = (v / pair_total for v in (lead_mean, lead_row, lag_row))
    lag = gathered_total(kept_ref, came_refs, left_ref, stats_refs, columns)
    zero = jnp.zeros_like(lag)
    for group, member in members:
        weight = (lengths_ref[place ^ (4 * group + member)] - LAG).astype(jnp.float32)
        column = 16 * group + 2 * member
        lead = left_ref[:, column : column + 1] - lead_mean * weight
        leads = stats_refs[group][2 * member : 2 * member + 1, columns]
        lags = stats_refs[group][2 * member + 1 : 2 * member + 2, columns]
        zero = zero + lead * (leads / weight - lead_row)
        lag = lag + lead * (lags / weight - lag_row)
    out_ref[...] = lag / pair_total
    zero_ref[...] = zero


def finish_lag(lengths, left, stats, kept, came):
    return pl.pallas_call(
        finish_lag_kernel,
        in_specs=[SCALARS] + [WHOLE] * (2 + len(stats) + len(came)),
        out_specs=[WHOLE, WHOLE],
        out_shape=[shape(kept.shape), shape(kept.shape)],
        compiler_params=params(),
        name="finish_lag",
    )(lengths, left, kept, *stats, *came)


def finish_zero_kernel(lengths_ref, left_ref, between_ref, kept_ref, *refs):
    groups = len(refs) // 2
    stats_refs, came_refs, out_ref = refs[:groups], refs[groups:-1], refs[-1]
    columns = side_columns(kept_ref.shape[1], True)
    zero = gathered_total(kept_ref, came_refs, left_ref, stats_refs, columns)
    out_ref[...] = (zero + between_ref[...]) / pairs_of(lengths_ref, 4 * groups)


def finish_zero(lengths, left, stats, between, kept, came):
    return pl.pallas_call(
        finish_zero_kernel,
        in_specs=[SCALARS] + [WHOLE] * (3 + len(stats) + len(came)),
        out_specs=WHOLE,
        out_shape=shape(kept.shape),
        compiler_params=params(),
        name="finish_zero",
    )(lengths, left, between, kept, *stats, *came)


def exclusive(size, distance):
    return [(i, i ^ distance) for i in range(size)]


def local(coords, lengths, atom_pairs):
    feats = atom_pairs.shape[1]
    dp = lax.axis_size("dp")
    far = dp // 2
    block = feats // dp
    home = coords.shape[0]
    depth = round_up(home - LAG, DEPTH_UNIT)
    rows = round_up(max(home, depth + LAG), FRAME_TILE)

    def swap(array, axis, distance):
        return lax.ppermute(array, axis, exclusive(lax.axis_size(axis), distance))

    coords = pltpu.with_memory_space_constraint(jnp.transpose(coords, (1, 0, 2)), pltpu.HBM)
    features, stats = contacts_call(coords, lengths, atom_pairs, rows)
    common = [lengths, features, stats]
    half = feats // 2
    kept_shape, sent_shape = shape((feats, half)), shape((feats, half), jnp.int16)
    peer = swap(stats, "tile", 1)
    (sent_lag,) = gram_call(sent_lag_kernel, common, [], [sent_shape], depth, LONG)
    came_lag = swap(sent_lag, "tile", 1)
    sent_zero, chip = gram_call(
        sent_zero_kernel, common + [peer], [], [sent_shape, shape((8, feats))], depth, LONG
    )
    near = swap(chip, "dp", 1)
    came_zero = swap(sent_zero, "tile", 1)
    (kept_lag,) = gram_call(kept_lag_kernel, common, [sent_zero], [kept_shape], depth, LONG)
    keep_lag, sent_lag = near_call(kept_lag, [came_lag], stats, peer, block, "near_lag")
    came_lag = swap(sent_lag, "dp", 1)
    kept_zero, pair = gram_call(
        kept_zero_kernel,
        common + [chip, near],
        [sent_lag],
        [kept_shape, shape((16, feats))],
        depth,
        LONG,
    )
    keep_zero, sent_zero = near_call(kept_zero, [came_zero], stats, peer, block, "near_zero")
    came_zero = swap(sent_zero, "dp", 1)

    gathered = [pair] + [swap(pair, "dp", 2 * step) for step in range(1, far)]
    first = lax.axis_index("dp") * block
    left = [lax.dynamic_slice_in_dim(part, first, block, axis=1) for part in gathered]
    left = jnp.concatenate(left, axis=0).T

    kept_lag, *sent_lag = far_call(keep_lag, came_lag, chip, near, block, "far_lag")
    came_lag = [swap(s, "dp", 2 * (i + 1)) for i, s in enumerate(sent_lag)]
    kept_zero, *sent_zero = far_call(keep_zero, came_zero, chip, near, block, "far_zero")
    came_zero = [swap(s, "dp", 2 * (i + 1)) for i, s in enumerate(sent_zero)]
    cov_lag, between = finish_lag(lengths, left, gathered, kept_lag, came_lag)
    cov_zero = finish_zero(lengths, left, gathered, between, kept_zero, came_zero)
    return (cov_zero, cov_lag)


def solution(mesh):
    placed = (P(("groups", "dp", "tile"), None, None), P("groups"), P())
    return jax.shard_map(
        local,
        mesh=mesh,
        in_specs=placed,
        out_specs=(P(("groups", "dp"), "tile"), P(("groups", "dp"), "tile")),
        check_vma=False,
    )
```

```python
import functools

import jax
import jax.numpy as jnp
from jax import lax
from jax.experimental import pallas as pl
from jax.experimental.pallas import tpu as pltpu
from jax.sharding import PartitionSpec as P

LAG = 500
FRAME_TILE = 512
FEATURE_TILE = 256
DEPTH_UNIT = 256
SLOPE = 6.0 * 1.4426950408889634
LEVELS = 32752.0
SLACK = 2e-5
FLOOR = 1e-36
PART = 32000.0
INVERSE_LOG_TWO = 1.4426950408889634
TAIL = 16
LONG = 1 << 34
SHORT = 1 << 20
SPLIT = 4
VMEM = 12 * 1024 * 1024
WHOLE = pl.BlockSpec(memory_space=pltpu.VMEM)
SCALARS = pl.BlockSpec(memory_space=pltpu.SMEM)


def round_up(value, unit):
    return -(-value // unit) * unit


def own_place():
    return lax.axis_index("dp") * lax.axis_size("tile") + lax.axis_index("tile")


def params():
    return pltpu.CompilerParams(vmem_limit_bytes=VMEM)


def shape(dims, dtype=jnp.float32):
    return jax.ShapeDtypeStruct(dims, dtype)


def to_levels(ratio):
    root = lax.rsqrt(jnp.maximum(jnp.abs(ratio), 1e-30)) * LEVELS
    return jnp.round(ratio * root).astype(jnp.int32).astype(jnp.int16)


def parts_of(block):
    return block.astype(jnp.int32).astype(jnp.float32)


def from_levels(block):
    level = parts_of(block)
    return level * jnp.abs(level)


def encode(vectors):
    half = vectors[0].shape[1] // 2
    rows, exponents = [], []
    for vector in vectors:
        top = jnp.maximum(jnp.max(vector, axis=1, keepdims=True), 1e-37)
        exponent = jnp.ceil(jnp.log(top) * INVERSE_LOG_TWO) + 1.0
        units = vector * (jnp.exp2(-exponent) * PART)
        high = jnp.floor(units)
        low = jnp.floor((units - high) * PART)
        rows += [high[:, :half], high[:, half:], low[:, :half], low[:, half:]]
        exponents.append(jnp.broadcast_to(exponent, (1, half)))
    rows = rows + exponents + exponents[:1]
    return jnp.concatenate(rows, axis=0).astype(jnp.int32).astype(jnp.int16)


def decode(block):
    parts = parts_of(block)
    vectors = []
    for index in range(3):
        first = 4 * index
        high = jnp.concatenate([parts[first : first + 1], parts[first + 1 : first + 2]], axis=1)
        low = jnp.concatenate([parts[first + 2 : first + 3], parts[first + 3 : first + 4]], axis=1)
        scale = jnp.exp2(parts[12 + index : 13 + index, 0:1]) * (1.0 / PART)
        vectors.append((high + low * (1.0 / PART)) * scale)
    return vectors


def live_of(lengths_ref, distances):
    place = own_place()
    total = 0
    for distance in distances:
        total = total + lengths_ref[place ^ distance] - LAG
    return total.astype(jnp.float32)


def pool(info_ref, sums, spread, count, other_block, other_count):
    lead, lag, deviation = decode(other_block)
    weight = count * other_count / (count + other_count)
    lead_step = sums[0] / count - lead / other_count
    lag_step = sums[1] / count - lag / other_count
    spread = spread + deviation * deviation + weight * (lead_step * lead_step + lag_step * lag_step)
    rows = [deviation, lead_step, lag_step, spread, sums[0] + lead, sums[1] + lag]
    info_ref[...] = jnp.concatenate(rows + rows[:2], axis=0)


def pooled_code(info_ref):
    return encode([info_ref[4:5, :], info_ref[5:6, :], jnp.sqrt(info_ref[3:4, :])])


def side_columns(half, own):
    side = lax.axis_index("tile")
    return pl.ds(pl.multiple_of((side if own else 1 - side) * half, half), half)


def load_right(features_ref, right_ref, own, lagged):
    depth, half = right_ref.shape
    first = LAG if lagged else 0
    right_ref[...] = features_ref[first : first + depth, side_columns(half, own)]


def gram_rows(features_ref, right_ref, start, live):
    depth = right_ref.shape[0]
    alive = lax.broadcasted_iota(jnp.int32, (depth, 1), 0) < live
    left = jnp.where(alive, features_ref[0:depth, start : start + FEATURE_TILE], 0.0)
    return lax.dot_general(
        left.astype(jnp.bfloat16),
        right_ref[...],
        (((0,), (0,)), ((), ())),
        preferred_element_type=jnp.float32,
    )


def contacts_kernel(
    lengths_ref, pairs_ref, coords_ref, features_ref, stats_ref, sent_ref, table_ref, right_ref
):
    step = pl.program_id(0)
    atoms, feats = table_ref.shape
    tile = coords_ref.shape[1]

    @pl.when(step == 0)
    def _():
        atom_ids = lax.broadcasted_iota(jnp.int32, (atoms, feats), 0)
        first_hit = (atom_ids == pairs_ref[0:1, :]).astype(jnp.float32)
        second_hit = (atom_ids == pairs_ref[1:2, :]).astype(jnp.float32)
        table_ref[...] = (first_hit - second_hit).astype(jnp.bfloat16)
        stats_ref[...] = jnp.zeros_like(stats_ref)

    live = lengths_ref[own_place()] - LAG
    frame = step * tile + lax.broadcasted_iota(jnp.int32, (tile, 1), 0)
    used = (frame < live) | ((frame >= LAG) & (frame < live + LAG))
    leads = (step * tile + tile <= live).astype(jnp.float32)
    target = pl.ds(pl.multiple_of(step * tile, tile), tile)
    for start in range(0, feats, FEATURE_TILE):
        columns = slice(start, start + FEATURE_TILE)
        weights = table_ref[:, columns]
        squared = None
        for axis in range(3):
            separation = jnp.dot(coords_ref[axis], weights, preferred_element_type=jnp.float32)
            square = separation * separation
            squared = square if squared is None else squared + square
        squared = jnp.maximum(squared, 1e-30)
        distance = squared * lax.rsqrt(squared)
        value = pl.reciprocal(1.0 + jnp.exp2(distance * SLOPE - SLOPE), approx=True)
        value = jnp.where(used, value, 0.0).astype(jnp.bfloat16)
        features_ref[target, columns] = value
        value = value.astype(jnp.float32)
        total = jnp.sum(value, axis=0, keepdims=True)
        stats_ref[0:1, columns] += total * leads
        stats_ref[2:3, columns] += total
        stats_ref[3:4, columns] += jnp.sum(value * value, axis=0, keepdims=True)

    @pl.when((step * tile < live) & (step * tile + tile > live))
    def _():
        value = jnp.where(frame < live, features_ref[target, :], 0.0).astype(jnp.float32)
        stats_ref[0:1, :] += jnp.sum(value, axis=0, keepdims=True)

    @pl.when(step == 0)
    def _():
        value = features_ref[0:LAG, :].astype(jnp.float32)
        stats_ref[1:2, :] = -jnp.sum(value, axis=0, keepdims=True)

    @pl.when(step == pl.num_programs(0) - 1)
    def _():
        count = live + jnp.minimum(live, LAG)
        total = stats_ref[2:3, :]
        squares = stats_ref[3:4, :]
        stats_ref[1:2, :] += total
        spread = squares - total * total / count.astype(jnp.float32)
        stats_ref[2:3, :] = jnp.maximum(spread, 0.0) + (SLACK * squares + FLOOR)
        gram_half(features_ref, stats_ref, [sent_ref], right_ref, live, False, True)
        sent_ref[feats : feats + TAIL, :] = encode(
            [stats_ref[0:1, :], stats_ref[1:2, :], jnp.sqrt(stats_ref[2:3, :])]
        )


def contacts_call(coords, lengths, atom_pairs, rows, depth):
    atoms = coords.shape[2]
    feats = atom_pairs.shape[1]
    return pl.pallas_call(
        contacts_kernel,
        grid=(rows // FRAME_TILE,),
        in_specs=[
            SCALARS,
            pl.BlockSpec((2, feats), lambda i: (0, 0)),
            pl.BlockSpec((3, FRAME_TILE, atoms), lambda i: (0, i, 0)),
        ],
        out_specs=[WHOLE, WHOLE, WHOLE],
        out_shape=[
            shape((rows, feats), jnp.bfloat16),
            shape((8, feats)),
            shape((feats + TAIL, feats // 2), jnp.int16),
        ],
        scratch_shapes=[
            pltpu.VMEM((atoms, feats), jnp.bfloat16),
            pltpu.VMEM((depth, feats // 2), jnp.bfloat16),
        ],
        compiler_params=params(),
        name="contacts_sent_lag",
    )(lengths, atom_pairs, coords)


def gram_half(features_ref, stats_ref, out_refs, right_ref, live, kept, lagged):
    half = out_refs[0].shape[1]
    feats = 2 * half
    part = feats // len(out_refs)
    load_right(features_ref, right_ref, kept, lagged)
    columns = side_columns(half, kept)
    right = 1 if lagged else 0
    left_stats = jnp.transpose(stats_ref[...])
    right_mean = stats_ref[right : right + 1, columns] / live.astype(jnp.float32)
    right_inverse = lax.rsqrt(stats_ref[2:3, columns])
    for start in range(0, feats, FEATURE_TILE):
        rows = slice(start, start + FEATURE_TILE)
        gram = gram_rows(features_ref, right_ref, start, live)
        gram = gram - left_stats[rows, 0:1] * right_mean
        if not kept:
            scale = lax.rsqrt(left_stats[rows, 2:3]) * right_inverse
            gram = to_levels(gram * scale)
        first = start % part
        out_refs[start // part][first : first + FEATURE_TILE, :] = gram


def kept_lag_kernel(lengths_ref, features_ref, stats_ref, _, kept_ref, right_ref):
    live = lengths_ref[own_place()] - LAG
    gram_half(features_ref, stats_ref, [kept_ref], right_ref, live, True, True)


def zero_kernel(lengths_ref, features_ref, stats_ref, _, *refs):
    sent_refs, kept_ref, right_ref = refs[:-2], refs[-2], refs[-1]
    live = lengths_ref[own_place()] - LAG
    gram_half(features_ref, stats_ref, sent_refs, right_ref, live, False, False)
    gram_half(features_ref, stats_ref, [kept_ref], right_ref, live, True, False)


def gram_call(body, operands, after, outs, depth, estimate):
    feats = operands[1].shape[1]
    return pl.pallas_call(
        body,
        in_specs=[SCALARS]
        + [WHOLE] * (len(operands) - 1)
        + [pl.BlockSpec(memory_space=pl.ANY)] * len(after),
        out_specs=[WHOLE] * len(outs),
        out_shape=outs,
        scratch_shapes=[pltpu.VMEM((depth, feats // 2), jnp.bfloat16)],
        compiler_params=params(),
        cost_estimate=pl.CostEstimate(flops=estimate, bytes_accessed=estimate // 1024, transcendentals=0),
        name=body.__name__.removesuffix("_kernel"),
    )(*operands, *after)


def near_kernel(lengths_ref, kept_ref, info_ref, *refs, lagged, block, parts):
    came_refs, keep_ref, sent_ref = refs[:parts], refs[parts], refs[parts + 1]
    near = lax.axis_index("dp") % 2
    feats, half = kept_ref.shape
    part = feats // parts
    columns = side_columns(half, True)
    count, peer_count = live_of(lengths_ref, [0]), live_of(lengths_ref, [1])
    if lagged:
        stats_ref, info_ref = info_ref, refs[-1]
        sums = (stats_ref[0:1, :], stats_ref[1:2, :])
        tail = came_refs[0][feats : feats + TAIL, :]
        pool(info_ref, sums, stats_ref[2:3, :], count, tail, peer_count)
        sent_ref[half : half + TAIL, :] = pooled_code(info_ref)
    weight = count * peer_count / (count + peer_count)
    left = jnp.transpose(info_ref[...])
    came_right = info_ref[0:1, columns] * (1.0 / LEVELS**2)
    step_right = info_ref[2 if lagged else 1 : 3 if lagged else 2, columns] * weight
    sent_right = lax.rsqrt(info_ref[3:4, columns])
    for start in range(0, feats, 2 * block):
        totals = []
        for rows in (slice(start, start + block), slice(start + block, start + 2 * block)):
            first = rows.start % part
            came = from_levels(came_refs[rows.start // part][first : first + block, :])
            total = kept_ref[rows, :] + came * (left[rows, 0:1] * came_right)
            totals.append(total + left[rows, 1:2] * step_right)
        target = slice(start // 2, start // 2 + block)
        keep_ref[target, :] = jnp.where(near == 0, totals[0], totals[1])
        other = jnp.where(near == 0, totals[1], totals[0])
        even = left[start : start + block, 3:4]
        odd = left[start + block : start + 2 * block, 3:4]
        spread = jnp.where(near == 0, odd, even)
        sent_ref[target, :] = to_levels(other * (lax.rsqrt(spread) * sent_right))


def near_call(lengths, kept, info, came, block, lagged):
    feats, half = kept.shape
    outs = [shape((half, half)), shape((half + (TAIL if lagged else 0), half), jnp.int16)]
    if lagged:
        outs.append(shape((8, feats)))
    return pl.pallas_call(
        functools.partial(near_kernel, lagged=lagged, block=block, parts=len(came)),
        in_specs=[SCALARS] + [WHOLE] * (2 + len(came)),
        out_specs=[WHOLE] * len(outs),
        out_shape=outs,
        compiler_params=params(),
        name="near_lag" if lagged else "near_zero",
    )(lengths, kept, info, *came)


def far_kernel(lengths_ref, keep_ref, came_ref, info_ref, *refs, lagged, block, far):
    kept_ref, sent_refs = refs[0], refs[1:far]
    total_ref, level_ref = refs[-2], refs[-1]
    place = lax.axis_index("dp")
    near, own_far = place % 2, place // 2
    half = keep_ref.shape[0]
    columns = side_columns(half, True)
    count, near_count = live_of(lengths_ref, [0, 1]), live_of(lengths_ref, [2, 3])
    if lagged:
        chip_ref, info_ref = info_ref, refs[far]
        sums = (chip_ref[4:5, :], chip_ref[5:6, :])
        pool(info_ref, sums, chip_ref[3:4, :], count, came_ref[half : half + TAIL, :], near_count)
        code = pooled_code(info_ref)
        for sent_ref in sent_refs:
            sent_ref[block : block + TAIL, :] = code
    weight = count * near_count / (count + near_count)
    left = jnp.transpose(info_ref[...])
    came_right = info_ref[0:1, columns] * (1.0 / LEVELS**2)
    step_right = info_ref[2 if lagged else 1 : 3 if lagged else 2, columns] * weight
    sent_right = lax.rsqrt(info_ref[3:4, columns])
    for index in range(far):
        rows = slice(index * block, (index + 1) * block)
        even = left[2 * index * block : (2 * index + 1) * block]
        odd = left[(2 * index + 1) * block : (2 * index + 2) * block]
        mine = jnp.where(near == 0, even, odd)
        total = keep_ref[rows, :] + from_levels(came_ref[rows, :]) * (mine[:, 0:1] * came_right)
        total = total + mine[:, 1:2] * step_right
        total_ref[index] = total
        level_ref[index] = to_levels(total * (lax.rsqrt(mine[:, 3:4]) * sent_right))
    kept_ref[...] = total_ref[own_far]
    for step, sent_ref in enumerate(sent_refs):
        sent_ref[0:block, :] = level_ref[own_far ^ (step + 1)]


def far_call(lengths, keep, came, info, block, lagged):
    half = keep.shape[0]
    far = half // block
    outs = [shape((block, half))]
    outs += [shape((block + (TAIL if lagged else 0), half), jnp.int16)] * (far - 1)
    if lagged:
        outs.append(shape(info.shape))
    estimate = LONG if lagged else SHORT
    return pl.pallas_call(
        functools.partial(far_kernel, lagged=lagged, block=block, far=far),
        in_specs=[SCALARS] + [WHOLE] * 3,
        out_specs=[WHOLE] * len(outs),
        out_shape=outs,
        scratch_shapes=[
            pltpu.VMEM((far, block, half), jnp.float32),
            pltpu.VMEM((far, block, half), jnp.int16),
        ],
        compiler_params=params(),
        cost_estimate=pl.CostEstimate(flops=estimate, bytes_accessed=estimate // 1024, transcendentals=0),
        name="far_lag" if lagged else "far_zero",
    )(lengths, keep, came, info)


def gathered_total(kept_ref, came_refs, rows_ref, left_ref, columns):
    block, far = kept_ref.shape[0], len(came_refs) + 1
    total = kept_ref[...]
    for index, came_ref in enumerate(came_refs):
        row = 2 * far + index
        right = rows_ref[row : row + 1, columns] * (1.0 / LEVELS**2)
        total = total + from_levels(came_ref[0:block, :]) * (left_ref[:, row : row + 1] * right)
    return total


def pairs_of(lengths_ref, members):
    total = lax.fori_loop(0, members, lambda i, t: t + lengths_ref[i] - LAG, 0)
    return total.astype(jnp.float32)


def finish_lag_kernel(lengths_ref, info_ref, kept_ref, *refs, far):
    came_refs = refs[: far - 1]
    out_ref, zero_ref, rows_ref, left_ref, turned_ref = refs[far - 1 :]
    block, half = kept_ref.shape
    columns = side_columns(half, True)
    found = [decode(came_ref[block : block + TAIL, :]) for came_ref in came_refs]
    rows = [info_ref[4:5, :]] + [f[0] for f in found] + [info_ref[5:6, :]] + [f[1] for f in found]
    rows += [f[2] for f in found]
    rows += [jnp.zeros_like(rows[0])] * (rows_ref.shape[0] - len(rows))
    rows_ref[...] = jnp.concatenate(rows, axis=0)
    turned_ref[...] = jnp.transpose(rows_ref[...])
    first = pl.multiple_of(lax.axis_index("dp") * block, block)
    left_ref[...] = turned_ref[pl.ds(first, block), :]
    pair_total = pairs_of(lengths_ref, lengths_ref.shape[0])
    lead_mean = lead_row = lag_row = 0.0
    for k in range(far):
        lead_mean += left_ref[:, k : k + 1]
        lead_row += rows_ref[k : k + 1, columns]
        lag_row += rows_ref[far + k : far + k + 1, columns]
    lead_mean, lead_row, lag_row = (v / pair_total for v in (lead_mean, lead_row, lag_row))
    lag = gathered_total(kept_ref, came_refs, rows_ref, left_ref, columns)
    zero = jnp.zeros_like(lag)
    for k in range(far):
        weight = live_of(lengths_ref, [4 * k + i for i in range(4)])
        lead = left_ref[:, k : k + 1] - lead_mean * weight
        zero = zero + lead * (rows_ref[k : k + 1, columns] / weight - lead_row)
        lag = lag + lead * (rows_ref[far + k : far + k + 1, columns] / weight - lag_row)
    out_ref[...] = lag / pair_total
    zero_ref[...] = zero


def finish_lag(lengths, info, kept, came):
    block, half = kept.shape
    feats = 2 * half
    far = len(came) + 1
    rows = round_up(3 * far - 1, 8)
    return pl.pallas_call(
        functools.partial(finish_lag_kernel, far=far),
        in_specs=[SCALARS] + [WHOLE] * (2 + len(came)),
        out_specs=[WHOLE] * 4,
        out_shape=[shape(kept.shape), shape(kept.shape), shape((rows, feats)), shape((block, rows))],
        scratch_shapes=[pltpu.VMEM((feats, rows), jnp.float32)],
        compiler_params=params(),
        name="finish_lag",
    )(lengths, info, kept, *came)


def finish_zero_kernel(lengths_ref, rows_ref, left_ref, between_ref, kept_ref, *refs):
    came_refs, out_ref = refs[:-1], refs[-1]
    columns = side_columns(kept_ref.shape[1], True)
    zero = gathered_total(kept_ref, came_refs, rows_ref, left_ref, columns)
    out_ref[...] = (zero + between_ref[...]) / pairs_of(lengths_ref, lengths_ref.shape[0])


def finish_zero(lengths, rows, left, between, kept, came):
    return pl.pallas_call(
        finish_zero_kernel,
        in_specs=[SCALARS] + [WHOLE] * (4 + len(came)),
        out_specs=WHOLE,
        out_shape=shape(kept.shape),
        compiler_params=params(),
        name="finish_zero",
    )(lengths, rows, left, between, kept, *came)


def exclusive(size, distance):
    return [(i, i ^ distance) for i in range(size)]


def local(coords, lengths, atom_pairs):
    feats = atom_pairs.shape[1]
    dp = lax.axis_size("dp")
    far = dp // 2
    block = feats // dp
    home = coords.shape[0]
    depth = round_up(home - LAG, DEPTH_UNIT)
    rows = round_up(max(home, depth + LAG), FRAME_TILE)

    def swap(array, axis, distance):
        return lax.ppermute(array, axis, exclusive(lax.axis_size(axis), distance))

    coords = pltpu.with_memory_space_constraint(jnp.transpose(coords, (1, 0, 2)), pltpu.HBM)
    atom_pairs = pltpu.with_memory_space_constraint(atom_pairs, pltpu.HBM)
    features, stats, sent_lag = contacts_call(coords, lengths, atom_pairs, rows, depth)
    common = [lengths, features, stats]
    half = feats // 2
    kept_shape = shape((feats, half))
    came_lag = swap(sent_lag, "tile", 1)
    (kept_lag,) = gram_call(kept_lag_kernel, common, [sent_lag], [kept_shape], depth, LONG)
    keep_lag, sent_lag, chip = near_call(lengths, kept_lag, stats, [came_lag], block, True)
    came_lag = swap(sent_lag, "dp", 1)
    *sent_zero, kept_zero = gram_call(
        zero_kernel,
        common,
        [sent_lag],
        [shape((feats // SPLIT, half), jnp.int16)] * SPLIT + [kept_shape],
        depth,
        SHORT,
    )
    came_zero = [swap(part, "tile", 1) for part in sent_zero]
    keep_zero, sent_zero = near_call(lengths, kept_zero, chip, came_zero, block, False)
    came_zero = swap(sent_zero, "dp", 1)

    kept_lag, *sent_lag, pair = far_call(lengths, keep_lag, came_lag, chip, block, True)
    came_lag = [swap(s, "dp", 2 * (i + 1)) for i, s in enumerate(sent_lag)]
    kept_zero, *sent_zero = far_call(lengths, keep_zero, came_zero, pair, block, False)
    came_zero = [swap(s, "dp", 2 * (i + 1)) for i, s in enumerate(sent_zero)]
    cov_lag, between, total_rows, total_left = finish_lag(lengths, pair, kept_lag, came_lag)
    cov_zero = finish_zero(lengths, total_rows, total_left, between, kept_zero, came_zero)
    return (cov_zero, cov_lag)


def solution(mesh):
    placed = (P(("groups", "dp", "tile"), None, None), P("groups"), P())
    return jax.shard_map(
        local,
        mesh=mesh,
        in_specs=placed,
        out_specs=(P(("groups", "dp"), "tile"), P(("groups", "dp"), "tile")),
        check_vma=False,
    )
```

```python
import functools

import jax
import jax.numpy as jnp
from jax import lax
from jax.experimental import pallas as pl
from jax.experimental.pallas import tpu as pltpu
from jax.sharding import PartitionSpec as P

LAG = 500
FRAME_TILE = 512
FEATURE_TILE = 256
DEPTH_UNIT = 256
SLOPE = 6.0 * 1.4426950408889634
LEVELS = 32752.0
SLACK = 2e-5
FLOOR = 1e-36
PART = 32000.0
INVERSE_LOG_TWO = 1.4426950408889634
TAIL = 16
LANES = 128
LONG = 1 << 34
SHORT = 1 << 20
SPLIT = 4
VMEM = 12 * 1024 * 1024
WHOLE = pl.BlockSpec(memory_space=pltpu.VMEM)
SCALARS = pl.BlockSpec(memory_space=pltpu.SMEM)


def round_up(value, unit):
    return -(-value // unit) * unit


def own_place():
    return lax.axis_index("dp") * lax.axis_size("tile") + lax.axis_index("tile")


def params():
    return pltpu.CompilerParams(vmem_limit_bytes=VMEM)


def shape(dims, dtype=jnp.float32):
    return jax.ShapeDtypeStruct(dims, dtype)


def to_levels(ratio):
    root = lax.rsqrt(jnp.maximum(jnp.abs(ratio), 1e-30)) * LEVELS
    return jnp.round(ratio * root).astype(jnp.int32).astype(jnp.int16)


def parts_of(block):
    return block.astype(jnp.int32).astype(jnp.float32)


def from_levels(block):
    level = parts_of(block)
    return level * jnp.abs(level)


def encode(vectors):
    half = vectors[0].shape[1] // 2
    rows, exponents = [], []
    for vector in vectors:
        top = jnp.maximum(jnp.max(vector, axis=1, keepdims=True), 1e-37)
        exponent = jnp.ceil(jnp.log(top) * INVERSE_LOG_TWO) + 1.0
        units = vector * (jnp.exp2(-exponent) * PART)
        high = jnp.floor(units)
        low = jnp.floor((units - high) * PART)
        rows += [high[:, :half], high[:, half:], low[:, :half], low[:, half:]]
        exponents.append(jnp.broadcast_to(exponent, (1, half)))
    rows = rows + exponents + exponents[:1]
    return jnp.concatenate(rows, axis=0).astype(jnp.int32).astype(jnp.int16)


def decode(block):
    parts = parts_of(block)
    vectors = []
    for index in range(3):
        first = 4 * index
        high = jnp.concatenate([parts[first : first + 1], parts[first + 1 : first + 2]], axis=1)
        low = jnp.concatenate([parts[first + 2 : first + 3], parts[first + 3 : first + 4]], axis=1)
        scale = jnp.exp2(parts[12 + index : 13 + index, 0:1]) * (1.0 / PART)
        vectors.append((high + low * (1.0 / PART)) * scale)
    return vectors


def count_pairs(lengths_ref, counts_ref):
    place = own_place()
    lane = lax.broadcasted_iota(jnp.int32, (1, counts_ref.shape[1]), 1)
    counts = jnp.zeros(lane.shape, jnp.float32)
    total = 0
    for distance in range(lengths_ref.shape[0]):
        live = lengths_ref[place ^ distance] - LAG
        counts = jnp.where(lane == distance, live.astype(jnp.float32), counts)
        total = total + live
    counts_ref[0:1, :] = counts
    counts_ref[1:8, :] = jnp.broadcast_to(total.astype(jnp.float32), (7, counts_ref.shape[1]))


def live_of(counts_ref, distances):
    return sum(counts_ref[0:1, d : d + 1] for d in distances)


def pool(info_ref, sums, spread, count, other_block, other_count):
    lead, lag, deviation = decode(other_block)
    weight = count * other_count / (count + other_count)
    lead_step = sums[0] / count - lead / other_count
    lag_step = sums[1] / count - lag / other_count
    spread = spread + deviation * deviation + weight * (lead_step * lead_step + lag_step * lag_step)
    rows = [deviation, lead_step, lag_step, spread, sums[0] + lead, sums[1] + lag]
    info_ref[...] = jnp.concatenate(rows + rows[:2], axis=0)


def pooled_code(info_ref):
    return encode([info_ref[4:5, :], info_ref[5:6, :], jnp.sqrt(info_ref[3:4, :])])


def side_columns(half, own):
    side = lax.axis_index("tile")
    return pl.ds(pl.multiple_of((side if own else 1 - side) * half, half), half)


def load_right(features_ref, right_ref, own, lagged):
    depth, half = right_ref.shape
    first = LAG if lagged else 0
    right_ref[...] = features_ref[first : first + depth, side_columns(half, own)]


def gram_rows(features_ref, right_ref, start, live):
    depth = right_ref.shape[0]
    alive = lax.broadcasted_iota(jnp.int32, (depth, 1), 0).astype(jnp.float32) < live
    left = jnp.where(alive, features_ref[0:depth, start : start + FEATURE_TILE], 0.0)
    return lax.dot_general(
        left.astype(jnp.bfloat16),
        right_ref[...],
        (((0,), (0,)), ((), ())),
        preferred_element_type=jnp.float32,
    )


def contacts_kernel(
    lengths_ref, pairs_ref, coords_ref, features_ref, stats_ref, sent_ref, counts_ref, table_ref, right_ref
):
    step = pl.program_id(0)
    atoms, feats = table_ref.shape
    tile = coords_ref.shape[1]

    @pl.when(step == 0)
    def _():
        atom_ids = lax.broadcasted_iota(jnp.int32, (atoms, feats), 0)
        first_hit = (atom_ids == pairs_ref[0:1, :]).astype(jnp.float32)
        second_hit = (atom_ids == pairs_ref[1:2, :]).astype(jnp.float32)
        table_ref[...] = (first_hit - second_hit).astype(jnp.bfloat16)
        stats_ref[...] = jnp.zeros_like(stats_ref)
        count_pairs(lengths_ref, counts_ref)

    live = lengths_ref[own_place()] - LAG
    frame = step * tile + lax.broadcasted_iota(jnp.int32, (tile, 1), 0)
    used = (frame < live) | ((frame >= LAG) & (frame < live + LAG))
    leads = (step * tile + tile <= live).astype(jnp.float32)
    target = pl.ds(pl.multiple_of(step * tile, tile), tile)
    for start in range(0, feats, FEATURE_TILE):
        columns = slice(start, start + FEATURE_TILE)
        weights = table_ref[:, columns]
        squared = None
        for axis in range(3):
            separation = jnp.dot(coords_ref[axis], weights, preferred_element_type=jnp.float32)
            square = separation * separation
            squared = square if squared is None else squared + square
        squared = jnp.maximum(squared, 1e-30)
        distance = squared * lax.rsqrt(squared)
        value = pl.reciprocal(1.0 + jnp.exp2(distance * SLOPE - SLOPE), approx=True)
        value = jnp.where(used, value, 0.0).astype(jnp.bfloat16)
        features_ref[target, columns] = value
        value = value.astype(jnp.float32)
        total = jnp.sum(value, axis=0, keepdims=True)
        stats_ref[0:1, columns] += total * leads
        stats_ref[2:3, columns] += total
        stats_ref[3:4, columns] += jnp.sum(value * value, axis=0, keepdims=True)

    @pl.when((step * tile < live) & (step * tile + tile > live))
    def _():
        value = jnp.where(frame < live, features_ref[target, :], 0.0).astype(jnp.float32)
        stats_ref[0:1, :] += jnp.sum(value, axis=0, keepdims=True)

    @pl.when(step == 0)
    def _():
        value = features_ref[0:LAG, :].astype(jnp.float32)
        stats_ref[1:2, :] = -jnp.sum(value, axis=0, keepdims=True)

    @pl.when(step == pl.num_programs(0) - 1)
    def _():
        count = live + jnp.minimum(live, LAG)
        total = stats_ref[2:3, :]
        squares = stats_ref[3:4, :]
        stats_ref[1:2, :] += total
        spread = squares - total * total / count.astype(jnp.float32)
        stats_ref[2:3, :] = jnp.maximum(spread, 0.0) + (SLACK * squares + FLOOR)
        gram_half(counts_ref, features_ref, stats_ref, [sent_ref], right_ref, False, True)
        sent_ref[feats : feats + TAIL, :] = encode(
            [stats_ref[0:1, :], stats_ref[1:2, :], jnp.sqrt(stats_ref[2:3, :])]
        )


def contacts_call(coords, lengths, atom_pairs, rows, depth):
    atoms = coords.shape[2]
    feats = atom_pairs.shape[1]
    return pl.pallas_call(
        contacts_kernel,
        grid=(rows // FRAME_TILE,),
        in_specs=[
            SCALARS,
            pl.BlockSpec((2, feats), lambda i: (0, 0)),
            pl.BlockSpec((3, FRAME_TILE, atoms), lambda i: (0, i, 0)),
        ],
        out_specs=[WHOLE] * 4,
        out_shape=[
            shape((rows, feats), jnp.bfloat16),
            shape((8, feats)),
            shape((feats + TAIL, feats // 2), jnp.int16),
            shape((8, LANES)),
        ],
        scratch_shapes=[
            pltpu.VMEM((atoms, feats), jnp.bfloat16),
            pltpu.VMEM((depth, feats // 2), jnp.bfloat16),
        ],
        compiler_params=params(),
        name="contacts_sent_lag",
    )(lengths, atom_pairs, coords)


def gram_half(counts_ref, features_ref, stats_ref, out_refs, right_ref, kept, lagged):
    half = out_refs[0].shape[1]
    feats = 2 * half
    part = feats // len(out_refs)
    load_right(features_ref, right_ref, kept, lagged)
    columns = side_columns(half, kept)
    right = 1 if lagged else 0
    left_stats = jnp.transpose(stats_ref[...])
    live = live_of(counts_ref, [0])
    right_mean = stats_ref[right : right + 1, columns] / live
    right_inverse = lax.rsqrt(stats_ref[2:3, columns])
    for start in range(0, feats, FEATURE_TILE):
        rows = slice(start, start + FEATURE_TILE)
        gram = gram_rows(features_ref, right_ref, start, live)
        gram = gram - left_stats[rows, 0:1] * right_mean
        if not kept:
            scale = lax.rsqrt(left_stats[rows, 2:3]) * right_inverse
            gram = to_levels(gram * scale)
        first = start % part
        out_refs[start // part][first : first + FEATURE_TILE, :] = gram


def kept_lag_kernel(counts_ref, features_ref, stats_ref, _, kept_ref, right_ref):
    gram_half(counts_ref, features_ref, stats_ref, [kept_ref], right_ref, True, True)


def zero_kernel(counts_ref, features_ref, stats_ref, _, *refs):
    sent_refs, kept_ref, right_ref = refs[:-2], refs[-2], refs[-1]
    gram_half(counts_ref, features_ref, stats_ref, sent_refs, right_ref, False, False)
    gram_half(counts_ref, features_ref, stats_ref, [kept_ref], right_ref, True, False)


def gram_call(body, operands, after, outs, depth, estimate):
    feats = operands[1].shape[1]
    return pl.pallas_call(
        body,
        in_specs=[WHOLE] * len(operands)
        + [pl.BlockSpec(memory_space=pl.ANY)] * len(after),
        out_specs=[WHOLE] * len(outs),
        out_shape=outs,
        scratch_shapes=[pltpu.VMEM((depth, feats // 2), jnp.bfloat16)],
        compiler_params=params(),
        cost_estimate=pl.CostEstimate(flops=estimate, bytes_accessed=estimate // 1024, transcendentals=0),
        name=body.__name__.removesuffix("_kernel"),
    )(*operands, *after)


def near_kernel(counts_ref, kept_ref, info_ref, *refs, lagged, block, parts):
    came_refs, keep_ref, sent_ref = refs[:parts], refs[parts], refs[parts + 1]
    near = lax.axis_index("dp") % 2
    feats, half = kept_ref.shape
    part = feats // parts
    columns = side_columns(half, True)
    count, peer_count = live_of(counts_ref, [0]), live_of(counts_ref, [1])
    if lagged:
        stats_ref, info_ref = info_ref, refs[-1]
        sums = (stats_ref[0:1, :], stats_ref[1:2, :])
        tail = came_refs[0][feats : feats + TAIL, :]
        pool(info_ref, sums, stats_ref[2:3, :], count, tail, peer_count)
        sent_ref[half : half + TAIL, :] = pooled_code(info_ref)
    weight = count * peer_count / (count + peer_count)
    left = jnp.transpose(info_ref[...])
    came_right = info_ref[0:1, columns] * (1.0 / LEVELS**2)
    step_right = info_ref[2 if lagged else 1 : 3 if lagged else 2, columns] * weight
    sent_right = lax.rsqrt(info_ref[3:4, columns])
    for start in range(0, feats, 2 * block):
        totals = []
        for rows in (slice(start, start + block), slice(start + block, start + 2 * block)):
            first = rows.start % part
            came = from_levels(came_refs[rows.start // part][first : first + block, :])
            total = kept_ref[rows, :] + came * (left[rows, 0:1] * came_right)
            totals.append(total + left[rows, 1:2] * step_right)
        target = slice(start // 2, start // 2 + block)
        keep_ref[target, :] = jnp.where(near == 0, totals[0], totals[1])
        other = jnp.where(near == 0, totals[1], totals[0])
        even = left[start : start + block, 3:4]
        odd = left[start + block : start + 2 * block, 3:4]
        spread = jnp.where(near == 0, odd, even)
        sent_ref[target, :] = to_levels(other * (lax.rsqrt(spread) * sent_right))


def near_call(counts, kept, info, came, block, lagged):
    feats, half = kept.shape
    outs = [shape((half, half)), shape((half + (TAIL if lagged else 0), half), jnp.int16)]
    if lagged:
        outs.append(shape((8, feats)))
    return pl.pallas_call(
        functools.partial(near_kernel, lagged=lagged, block=block, parts=len(came)),
        in_specs=[WHOLE] * (3 + len(came)),
        out_specs=[WHOLE] * len(outs),
        out_shape=outs,
        compiler_params=params(),
        name="near_lag" if lagged else "near_zero",
    )(counts, kept, info, *came)


def far_kernel(counts_ref, keep_ref, came_ref, info_ref, *refs, lagged, block, far):
    kept_ref, sent_refs = refs[0], refs[1:far]
    total_ref, level_ref = refs[-2], refs[-1]
    place = lax.axis_index("dp")
    near, own_far = place % 2, place // 2
    half = keep_ref.shape[0]
    columns = side_columns(half, True)
    count, near_count = live_of(counts_ref, [0, 1]), live_of(counts_ref, [2, 3])
    if lagged:
        chip_ref, info_ref = info_ref, refs[far]
        sums = (chip_ref[4:5, :], chip_ref[5:6, :])
        pool(info_ref, sums, chip_ref[3:4, :], count, came_ref[half : half + TAIL, :], near_count)
        code = pooled_code(info_ref)
        for sent_ref in sent_refs:
            sent_ref[block : block + TAIL, :] = code
    weight = count * near_count / (count + near_count)
    left = jnp.transpose(info_ref[...])
    came_right = info_ref[0:1, columns] * (1.0 / LEVELS**2)
    step_right = info_ref[2 if lagged else 1 : 3 if lagged else 2, columns] * weight
    sent_right = lax.rsqrt(info_ref[3:4, columns])
    for index in range(far):
        rows = slice(index * block, (index + 1) * block)
        even = left[2 * index * block : (2 * index + 1) * block]
        odd = left[(2 * index + 1) * block : (2 * index + 2) * block]
        mine = jnp.where(near == 0, even, odd)
        total = keep_ref[rows, :] + from_levels(came_ref[rows, :]) * (mine[:, 0:1] * came_right)
        total = total + mine[:, 1:2] * step_right
        total_ref[index] = total
        level_ref[index] = to_levels(total * (lax.rsqrt(mine[:, 3:4]) * sent_right))
    kept_ref[...] = total_ref[own_far]
    for step, sent_ref in enumerate(sent_refs):
        sent_ref[0:block, :] = level_ref[own_far ^ (step + 1)]


def far_call(counts, keep, came, info, block, lagged):
    half = keep.shape[0]
    far = half // block
    outs = [shape((block, half))]
    outs += [shape((block + (TAIL if lagged else 0), half), jnp.int16)] * (far - 1)
    if lagged:
        outs.append(shape(info.shape))
    estimate = LONG if lagged else SHORT
    return pl.pallas_call(
        functools.partial(far_kernel, lagged=lagged, block=block, far=far),
        in_specs=[WHOLE] * 4,
        out_specs=[WHOLE] * len(outs),
        out_shape=outs,
        scratch_shapes=[
            pltpu.VMEM((far, block, half), jnp.float32),
            pltpu.VMEM((far, block, half), jnp.int16),
        ],
        compiler_params=params(),
        cost_estimate=pl.CostEstimate(flops=estimate, bytes_accessed=estimate // 1024, transcendentals=0),
        name="far_lag" if lagged else "far_zero",
    )(counts, keep, came, info)


def first_last(items):
    return [*items[1:], *items[:1]]


def last_first(items):
    return [*items[-1:], *items[:-1]]


def gathered_total(kept_ref, came_refs, rows_ref, left_ref, columns):
    block, far = kept_ref.shape[0], len(came_refs) + 1
    total = kept_ref[...]
    for index, came_ref in enumerate(came_refs):
        row = 2 * far + index
        right = rows_ref[row : row + 1, columns] * (1.0 / LEVELS**2)
        total = total + from_levels(came_ref[0:block, :]) * (left_ref[:, row : row + 1] * right)
    return total


def finish_lag_kernel(counts_ref, info_ref, kept_ref, *refs, far):
    came_refs = last_first(refs[: far - 1])
    out_ref, zero_ref, rows_ref, left_ref, turned_ref = refs[far - 1 :]
    block, half = kept_ref.shape
    columns = side_columns(half, True)
    found = [decode(came_ref[block : block + TAIL, :]) for came_ref in came_refs]
    rows = [info_ref[4:5, :]] + [f[0] for f in found] + [info_ref[5:6, :]] + [f[1] for f in found]
    rows += [f[2] for f in found]
    rows += [jnp.zeros_like(rows[0])] * (rows_ref.shape[0] - len(rows))
    rows_ref[...] = jnp.concatenate(rows, axis=0)
    turned_ref[...] = jnp.transpose(rows_ref[...])
    first = pl.multiple_of(lax.axis_index("dp") * block, block)
    left_ref[...] = turned_ref[pl.ds(first, block), :]
    pair_total = counts_ref[1:2, 0:1]
    lead_mean = lead_row = lag_row = 0.0
    for k in range(far):
        lead_mean += left_ref[:, k : k + 1]
        lead_row += rows_ref[k : k + 1, columns]
        lag_row += rows_ref[far + k : far + k + 1, columns]
    lead_mean, lead_row, lag_row = (v / pair_total for v in (lead_mean, lead_row, lag_row))
    lag = gathered_total(kept_ref, came_refs, rows_ref, left_ref, columns)
    zero = jnp.zeros_like(lag)
    for k in range(far):
        weight = live_of(counts_ref, [4 * k + i for i in range(4)])
        lead = left_ref[:, k : k + 1] - lead_mean * weight
        zero = zero + lead * (rows_ref[k : k + 1, columns] / weight - lead_row)
        lag = lag + lead * (rows_ref[far + k : far + k + 1, columns] / weight - lag_row)
    out_ref[...] = lag / pair_total
    zero_ref[...] = zero


def finish_lag(counts, info, kept, came):
    block, half = kept.shape
    feats = 2 * half
    far = len(came) + 1
    rows = round_up(3 * far - 1, 8)
    return pl.pallas_call(
        functools.partial(finish_lag_kernel, far=far),
        in_specs=[WHOLE] * (3 + len(came)),
        out_specs=[WHOLE] * 4,
        out_shape=[shape(kept.shape), shape(kept.shape), shape((rows, feats)), shape((block, rows))],
        scratch_shapes=[pltpu.VMEM((feats, rows), jnp.float32)],
        compiler_params=params(),
        name="finish_lag",
    )(counts, info, kept, *first_last(came))


def finish_zero_kernel(counts_ref, rows_ref, left_ref, between_ref, kept_ref, *refs):
    came_refs, out_ref = last_first(refs[:-1]), refs[-1]
    columns = side_columns(kept_ref.shape[1], True)
    zero = gathered_total(kept_ref, came_refs, rows_ref, left_ref, columns)
    out_ref[...] = (zero + between_ref[...]) / counts_ref[1:2, 0:1]


def finish_zero(counts, rows, left, between, kept, came):
    return pl.pallas_call(
        finish_zero_kernel,
        in_specs=[WHOLE] * (5 + len(came)),
        out_specs=WHOLE,
        out_shape=shape(kept.shape),
        compiler_params=params(),
        name="finish_zero",
    )(counts, rows, left, between, kept, *first_last(came))


def exclusive(size, distance):
    return [(i, i ^ distance) for i in range(size)]


def local(coords, lengths, atom_pairs):
    feats = atom_pairs.shape[1]
    dp = lax.axis_size("dp")
    far = dp // 2
    block = feats // dp
    home = coords.shape[0]
    depth = round_up(home - LAG, DEPTH_UNIT)
    rows = round_up(max(home, depth + LAG), FRAME_TILE)

    def swap(array, axis, distance):
        return lax.ppermute(array, axis, exclusive(lax.axis_size(axis), distance))

    coords = pltpu.with_memory_space_constraint(jnp.transpose(coords, (1, 0, 2)), pltpu.HBM)
    atom_pairs = pltpu.with_memory_space_constraint(atom_pairs, pltpu.HBM)
    lengths = pltpu.with_memory_space_constraint(lengths, pltpu.HBM)
    features, stats, sent_lag, counts = contacts_call(coords, lengths, atom_pairs, rows, depth)
    common = [counts, features, stats]
    half = feats // 2
    kept_shape = shape((feats, half))
    came_lag = swap(sent_lag, "tile", 1)
    (kept_lag,) = gram_call(kept_lag_kernel, common, [sent_lag], [kept_shape], depth, LONG)
    keep_lag, sent_lag, chip = near_call(counts, kept_lag, stats, [came_lag], block, True)
    came_lag = swap(sent_lag, "dp", 1)
    *sent_zero, kept_zero = gram_call(
        zero_kernel,
        common,
        [sent_lag],
        [shape((feats // SPLIT, half), jnp.int16)] * SPLIT + [kept_shape],
        depth,
        SHORT,
    )
    came_zero = [swap(part, "tile", 1) for part in sent_zero]
    keep_zero, sent_zero = near_call(counts, kept_zero, chip, came_zero, block, False)
    came_zero = swap(sent_zero, "dp", 1)

    kept_lag, *sent_lag, pair = far_call(counts, keep_lag, came_lag, chip, block, True)
    came_lag = [swap(s, "dp", 2 * (i + 1)) for i, s in enumerate(sent_lag)]
    kept_zero, *sent_zero = far_call(counts, keep_zero, came_zero, pair, block, False)
    came_zero = [swap(s, "dp", 2 * (i + 1)) for i, s in enumerate(sent_zero)]
    cov_lag, between, total_rows, total_left = finish_lag(counts, pair, kept_lag, came_lag)
    cov_zero = finish_zero(counts, total_rows, total_left, between, kept_zero, came_zero)
    return (cov_zero, cov_lag)


def solution(mesh):
    placed = (P(("groups", "dp", "tile"), None, None), P("groups"), P())
    return jax.shard_map(
        local,
        mesh=mesh,
        in_specs=placed,
        out_specs=(P(("groups", "dp"), "tile"), P(("groups", "dp"), "tile")),
        check_vma=False,
    )
```

```python
import functools

import jax
import jax.numpy as jnp
from jax import lax
from jax.experimental import pallas as pl
from jax.experimental.pallas import tpu as pltpu
from jax.sharding import PartitionSpec as P

LAG = 500
FRAME_TILE = 512
FEATURE_TILE = 256
DEPTH_UNIT = 256
SLOPE = 6.0 * 1.4426950408889634
LEVELS = 32752.0
SLACK = 2e-5
FLOOR = 1e-36
PART = 32000.0
INVERSE_LOG_TWO = 1.4426950408889634
TAIL = 16
LANES = 128
LONG = 1 << 34
SHORT = 1 << 20
SPLIT = 4
VMEM = 12 * 1024 * 1024
WHOLE = pl.BlockSpec(memory_space=pltpu.VMEM)
SCALARS = pl.BlockSpec(memory_space=pltpu.SMEM)


def round_up(value, unit):
    return -(-value // unit) * unit


def own_place():
    return lax.axis_index("dp") * lax.axis_size("tile") + lax.axis_index("tile")


def params():
    return pltpu.CompilerParams(vmem_limit_bytes=VMEM)


def shape(dims, dtype=jnp.float32):
    return jax.ShapeDtypeStruct(dims, dtype)


def to_levels(ratio):
    root = lax.rsqrt(jnp.maximum(jnp.abs(ratio), 1e-30)) * LEVELS
    return jnp.round(ratio * root).astype(jnp.int32).astype(jnp.int16)


def parts_of(block):
    return block.astype(jnp.int32).astype(jnp.float32)


def from_levels(block):
    level = parts_of(block)
    return level * jnp.abs(level)


def encode(vectors):
    half = vectors[0].shape[1] // 2
    rows, exponents = [], []
    for vector in vectors:
        top = jnp.maximum(jnp.max(vector, axis=1, keepdims=True), 1e-37)
        exponent = jnp.ceil(jnp.log(top) * INVERSE_LOG_TWO) + 1.0
        units = vector * (jnp.exp2(-exponent) * PART)
        high = jnp.floor(units)
        low = jnp.floor((units - high) * PART)
        rows += [high[:, :half], high[:, half:], low[:, :half], low[:, half:]]
        exponents.append(jnp.broadcast_to(exponent, (1, half)))
    rows = rows + exponents + exponents[:1]
    return jnp.concatenate(rows, axis=0).astype(jnp.int32).astype(jnp.int16)


def decode(block):
    parts = parts_of(block)
    vectors = []
    for index in range(3):
        first = 4 * index
        high = jnp.concatenate([parts[first : first + 1], parts[first + 1 : first + 2]], axis=1)
        low = jnp.concatenate([parts[first + 2 : first + 3], parts[first + 3 : first + 4]], axis=1)
        scale = jnp.exp2(parts[12 + index : 13 + index, 0:1]) * (1.0 / PART)
        vectors.append((high + low * (1.0 / PART)) * scale)
    return vectors


def count_pairs(lengths_ref, counts_ref):
    place = own_place()
    lane = lax.broadcasted_iota(jnp.int32, (1, counts_ref.shape[1]), 1)
    counts = jnp.zeros(lane.shape, jnp.float32)
    total = 0
    for distance in range(lengths_ref.shape[0]):
        live = lengths_ref[place ^ distance] - LAG
        counts = jnp.where(lane == distance, live.astype(jnp.float32), counts)
        total = total + live
    counts_ref[0:1, :] = counts
    counts_ref[1:8, :] = jnp.broadcast_to(total.astype(jnp.float32), (7, counts_ref.shape[1]))


def live_of(counts_ref, distances):
    return sum(counts_ref[0:1, d : d + 1] for d in distances)


def pool(info_ref, sums, spread, count, other_block, other_count):
    lead, lag, deviation = decode(other_block)
    weight = count * other_count / (count + other_count)
    lead_step = sums[0] / count - lead / other_count
    lag_step = sums[1] / count - lag / other_count
    spread = spread + deviation * deviation + weight * (lead_step * lead_step + lag_step * lag_step)
    rows = [deviation, lead_step, lag_step, spread, sums[0] + lead, sums[1] + lag]
    info_ref[...] = jnp.concatenate(rows + rows[:2], axis=0)


def pooled_code(info_ref):
    return encode([info_ref[4:5, :], info_ref[5:6, :], jnp.sqrt(info_ref[3:4, :])])


def side_columns(half, own):
    side = lax.axis_index("tile")
    return pl.ds(pl.multiple_of((side if own else 1 - side) * half, half), half)


def load_right(features_ref, right_ref, own, lagged):
    depth, half = right_ref.shape
    first = LAG if lagged else 0
    right_ref[...] = features_ref[first : first + depth, side_columns(half, own)]


def gram_rows(features_ref, right_ref, start, live):
    depth = right_ref.shape[0]
    alive = lax.broadcasted_iota(jnp.int32, (depth, 1), 0).astype(jnp.float32) < live
    left = jnp.where(alive, features_ref[0:depth, start : start + FEATURE_TILE], 0.0)
    return lax.dot_general(
        left.astype(jnp.bfloat16),
        right_ref[...],
        (((0,), (0,)), ((), ())),
        preferred_element_type=jnp.float32,
    )


def contacts_kernel(
    lengths_ref, pairs_ref, coords_ref, features_ref, stats_ref, sent_ref, counts_ref, table_ref, right_ref
):
    step = pl.program_id(0)
    atoms, feats = table_ref.shape
    tile = coords_ref.shape[1]

    @pl.when(step == 0)
    def _():
        atom_ids = lax.broadcasted_iota(jnp.int32, (atoms, feats), 0)
        first_hit = (atom_ids == pairs_ref[0:1, :]).astype(jnp.float32)
        second_hit = (atom_ids == pairs_ref[1:2, :]).astype(jnp.float32)
        table_ref[...] = (first_hit - second_hit).astype(jnp.bfloat16)
        stats_ref[...] = jnp.zeros_like(stats_ref)
        count_pairs(lengths_ref, counts_ref)

    live = lengths_ref[own_place()] - LAG
    frame = step * tile + lax.broadcasted_iota(jnp.int32, (tile, 1), 0)
    used = (frame < live) | ((frame >= LAG) & (frame < live + LAG))
    leads = (step * tile + tile <= live).astype(jnp.float32)
    target = pl.ds(pl.multiple_of(step * tile, tile), tile)
    for start in range(0, feats, FEATURE_TILE):
        columns = slice(start, start + FEATURE_TILE)
        weights = table_ref[:, columns]
        squared = None
        for axis in range(3):
            separation = jnp.dot(coords_ref[axis], weights, preferred_element_type=jnp.float32)
            square = separation * separation
            squared = square if squared is None else squared + square
        squared = jnp.maximum(squared, 1e-30)
        distance = squared * lax.rsqrt(squared)
        value = pl.reciprocal(1.0 + jnp.exp2(distance * SLOPE - SLOPE), approx=True)
        value = jnp.where(used, value, 0.0).astype(jnp.bfloat16)
        features_ref[target, columns] = value
        value = value.astype(jnp.float32)
        total = jnp.sum(value, axis=0, keepdims=True)
        stats_ref[0:1, columns] += total * leads
        stats_ref[2:3, columns] += total
        stats_ref[3:4, columns] += jnp.sum(value * value, axis=0, keepdims=True)

    @pl.when((step * tile < live) & (step * tile + tile > live))
    def _():
        value = jnp.where(frame < live, features_ref[target, :], 0.0).astype(jnp.float32)
        stats_ref[0:1, :] += jnp.sum(value, axis=0, keepdims=True)

    @pl.when(step == 0)
    def _():
        value = features_ref[0:LAG, :].astype(jnp.float32)
        stats_ref[1:2, :] = -jnp.sum(value, axis=0, keepdims=True)

    @pl.when(step == pl.num_programs(0) - 1)
    def _():
        count = live + jnp.minimum(live, LAG)
        total = stats_ref[2:3, :]
        squares = stats_ref[3:4, :]
        stats_ref[1:2, :] += total
        spread = squares - total * total / count.astype(jnp.float32)
        stats_ref[2:3, :] = jnp.maximum(spread, 0.0) + (SLACK * squares + FLOOR)
        gram_half(counts_ref, features_ref, stats_ref, [sent_ref], right_ref, False, True)
        sent_ref[feats : feats + TAIL, :] = encode(
            [stats_ref[0:1, :], stats_ref[1:2, :], jnp.sqrt(stats_ref[2:3, :])]
        )


def contacts_call(coords, lengths, atom_pairs, rows, depth):
    atoms = coords.shape[2]
    feats = atom_pairs.shape[1]
    return pl.pallas_call(
        contacts_kernel,
        grid=(rows // FRAME_TILE,),
        in_specs=[
            SCALARS,
            pl.BlockSpec((2, feats), lambda i: (0, 0)),
            pl.BlockSpec((3, FRAME_TILE, atoms), lambda i: (0, i, 0)),
        ],
        out_specs=[WHOLE] * 4,
        out_shape=[
            shape((rows, feats), jnp.bfloat16),
            shape((8, feats)),
            shape((feats + TAIL, feats // 2), jnp.int16),
            shape((8, LANES)),
        ],
        scratch_shapes=[
            pltpu.VMEM((atoms, feats), jnp.bfloat16),
            pltpu.VMEM((depth, feats // 2), jnp.bfloat16),
        ],
        compiler_params=params(),
        name="contacts_sent_lag",
    )(lengths, atom_pairs, coords)


def gram_half(counts_ref, features_ref, stats_ref, out_refs, right_ref, kept, lagged):
    half = out_refs[0].shape[1]
    feats = 2 * half
    part = feats // len(out_refs)
    load_right(features_ref, right_ref, kept, lagged)
    columns = side_columns(half, kept)
    right = 1 if lagged else 0
    left_stats = jnp.transpose(stats_ref[...])
    live = live_of(counts_ref, [0])
    right_mean = stats_ref[right : right + 1, columns] / live
    right_inverse = lax.rsqrt(stats_ref[2:3, columns])
    for start in range(0, feats, FEATURE_TILE):
        rows = slice(start, start + FEATURE_TILE)
        gram = gram_rows(features_ref, right_ref, start, live)
        gram = gram - left_stats[rows, 0:1] * right_mean
        if not kept:
            scale = lax.rsqrt(left_stats[rows, 2:3]) * right_inverse
            gram = to_levels(gram * scale)
        first = start % part
        out_refs[start // part][first : first + FEATURE_TILE, :] = gram


def chosen(own, even, odd):
    near = lax.axis_index("dp") % 2
    return jnp.where(near == 0, even, odd) if own else jnp.where(near == 0, odd, even)


def chosen_block(own, ref, index, block):
    first = 2 * index * block
    return chosen(own, ref[first : first + block, :], ref[first + block : first + 2 * block, :])


def kept_part(counts_ref, features_ref, stats_ref, right_ref, kept_ref, own, block):
    depth, half = right_ref.shape
    columns = side_columns(half, True)
    live = live_of(counts_ref, [0])
    left_total = jnp.transpose(stats_ref[...])[:, 0:1]
    right_mean = stats_ref[1:2, columns] / live
    alive = lax.broadcasted_iota(jnp.int32, (depth, 1), 0).astype(jnp.float32) < live
    for start in range(0, half, FEATURE_TILE):
        left, totals = [], []
        for first in range(2 * start, 2 * (start + FEATURE_TILE), 2 * block):
            even, odd = slice(first, first + block), slice(first + block, first + 2 * block)
            left.append(chosen(own, features_ref[0:depth, even], features_ref[0:depth, odd]))
            totals.append(chosen(own, left_total[even], left_total[odd]))
        left = jnp.where(alive, jnp.concatenate(left, axis=1), 0.0).astype(jnp.bfloat16)
        gram = lax.dot_general(
            left, right_ref[...], (((0,), (0,)), ((), ())), preferred_element_type=jnp.float32
        )
        total = jnp.concatenate(totals, axis=0)
        kept_ref[start : start + FEATURE_TILE, :] = gram - total * right_mean


def other_lag_kernel(counts_ref, features_ref, stats_ref, _, kept_ref, right_ref, *, block):
    load_right(features_ref, right_ref, True, True)
    kept_part(counts_ref, features_ref, stats_ref, right_ref, kept_ref, False, block)


def own_lag_kernel(counts_ref, features_ref, stats_ref, right_ref, _, kept_ref, *, block):
    kept_part(counts_ref, features_ref, stats_ref, right_ref, kept_ref, True, block)


def part_call(body, operands, after, outs, block, estimate, name):
    return pl.pallas_call(
        functools.partial(body, block=block),
        in_specs=[WHOLE] * len(operands) + [pl.BlockSpec(memory_space=pl.ANY)] * len(after),
        out_specs=[WHOLE] * len(outs),
        out_shape=outs,
        compiler_params=params(),
        cost_estimate=pl.CostEstimate(flops=estimate, bytes_accessed=estimate // 1024, transcendentals=0),
        name=name,
    )(*operands, *after)


def near_other_kernel(counts_ref, kept_ref, stats_ref, came_ref, sent_ref, info_ref, *, block):
    half = kept_ref.shape[0]
    feats = 2 * half
    columns = side_columns(half, True)
    count, peer_count = live_of(counts_ref, [0]), live_of(counts_ref, [1])
    sums = (stats_ref[0:1, :], stats_ref[1:2, :])
    pool(info_ref, sums, stats_ref[2:3, :], count, came_ref[feats : feats + TAIL, :], peer_count)
    sent_ref[half : half + TAIL, :] = pooled_code(info_ref)
    weight = count * peer_count / (count + peer_count)
    left = jnp.transpose(info_ref[...])
    came_right = info_ref[0:1, columns] * (1.0 / LEVELS**2)
    step_right = info_ref[2:3, columns] * weight
    sent_right = lax.rsqrt(info_ref[3:4, columns])
    for index in range(half // block):
        rows = slice(index * block, (index + 1) * block)
        mine = chosen_block(False, left, index, block)
        came = from_levels(chosen_block(False, came_ref, index, block))
        total = kept_ref[rows, :] + came * (mine[:, 0:1] * came_right) + mine[:, 1:2] * step_right
        sent_ref[rows, :] = to_levels(total * (lax.rsqrt(mine[:, 3:4]) * sent_right))


def near_own_kernel(counts_ref, kept_ref, info_ref, came_ref, keep_ref, *, block):
    half = kept_ref.shape[0]
    columns = side_columns(half, True)
    count, peer_count = live_of(counts_ref, [0]), live_of(counts_ref, [1])
    weight = count * peer_count / (count + peer_count)
    left = jnp.transpose(info_ref[...])
    came_right = info_ref[0:1, columns] * (1.0 / LEVELS**2)
    step_right = info_ref[2:3, columns] * weight
    for index in range(half // block):
        rows = slice(index * block, (index + 1) * block)
        mine = chosen_block(True, left, index, block)
        came = from_levels(chosen_block(True, came_ref, index, block))
        keep_ref[rows, :] = (
            kept_ref[rows, :] + came * (mine[:, 0:1] * came_right) + mine[:, 1:2] * step_right
        )


def sent_zero_kernel(counts_ref, features_ref, stats_ref, _, *refs):
    gram_half(counts_ref, features_ref, stats_ref, refs[:-1], refs[-1], False, False)


def kept_zero_kernel(counts_ref, features_ref, stats_ref, _, kept_ref, right_ref):
    gram_half(counts_ref, features_ref, stats_ref, [kept_ref], right_ref, True, False)


def gram_call(body, operands, after, outs, depth, estimate):
    feats = operands[1].shape[1]
    return pl.pallas_call(
        body,
        in_specs=[WHOLE] * len(operands)
        + [pl.BlockSpec(memory_space=pl.ANY)] * len(after),
        out_specs=[WHOLE] * len(outs),
        out_shape=outs,
        scratch_shapes=[pltpu.VMEM((depth, feats // 2), jnp.bfloat16)],
        compiler_params=params(),
        cost_estimate=pl.CostEstimate(flops=estimate, bytes_accessed=estimate // 1024, transcendentals=0),
        name=body.__name__.removesuffix("_kernel"),
    )(*operands, *after)


def near_zero_kernel(counts_ref, kept_ref, info_ref, *refs, own, block):
    came_refs, out_ref = refs[:-1], refs[-1]
    feats, half = kept_ref.shape
    part = feats // len(came_refs)
    columns = side_columns(half, True)
    count, peer_count = live_of(counts_ref, [0]), live_of(counts_ref, [1])
    weight = count * peer_count / (count + peer_count)
    left = jnp.transpose(info_ref[...])
    came_right = info_ref[0:1, columns] * (1.0 / LEVELS**2)
    step_right = info_ref[1:2, columns] * weight
    sent_right = lax.rsqrt(info_ref[3:4, columns])
    for index in range(half // block):
        mine = chosen_block(own, left, index, block)
        kept = chosen_block(own, kept_ref, index, block)
        came_ref, inside = came_refs[2 * index * block // part], 2 * index * block % part
        even, odd = came_ref[inside : inside + block, :], came_ref[inside + block : inside + 2 * block, :]
        came = from_levels(chosen(own, even, odd))
        total = kept + came * (mine[:, 0:1] * came_right) + mine[:, 1:2] * step_right
        if not own:
            total = to_levels(total * (lax.rsqrt(mine[:, 3:4]) * sent_right))
        out_ref[index * block : (index + 1) * block, :] = total


def far_kernel(counts_ref, keep_ref, came_ref, info_ref, *refs, lagged, block, far):
    kept_ref, sent_refs = refs[0], refs[1:far]
    total_ref, level_ref = refs[-2], refs[-1]
    place = lax.axis_index("dp")
    near, own_far = place % 2, place // 2
    half = keep_ref.shape[0]
    columns = side_columns(half, True)
    count, near_count = live_of(counts_ref, [0, 1]), live_of(counts_ref, [2, 3])
    if lagged:
        chip_ref, info_ref = info_ref, refs[far]
        sums = (chip_ref[4:5, :], chip_ref[5:6, :])
        pool(info_ref, sums, chip_ref[3:4, :], count, came_ref[half : half + TAIL, :], near_count)
        code = pooled_code(info_ref)
        for sent_ref in sent_refs:
            sent_ref[block : block + TAIL, :] = code
    weight = count * near_count / (count + near_count)
    left = jnp.transpose(info_ref[...])
    came_right = info_ref[0:1, columns] * (1.0 / LEVELS**2)
    step_right = info_ref[2 if lagged else 1 : 3 if lagged else 2, columns] * weight
    sent_right = lax.rsqrt(info_ref[3:4, columns])
    for index in range(far):
        rows = slice(index * block, (index + 1) * block)
        even = left[2 * index * block : (2 * index + 1) * block]
        odd = left[(2 * index + 1) * block : (2 * index + 2) * block]
        mine = jnp.where(near == 0, even, odd)
        total = keep_ref[rows, :] + from_levels(came_ref[rows, :]) * (mine[:, 0:1] * came_right)
        total = total + mine[:, 1:2] * step_right
        total_ref[index] = total
        level_ref[index] = to_levels(total * (lax.rsqrt(mine[:, 3:4]) * sent_right))
    kept_ref[...] = total_ref[own_far]
    for step, sent_ref in enumerate(sent_refs):
        sent_ref[0:block, :] = level_ref[own_far ^ (step + 1)]


def far_call(counts, keep, came, info, block, lagged):
    half = keep.shape[0]
    far = half // block
    outs = [shape((block, half))]
    outs += [shape((block + (TAIL if lagged else 0), half), jnp.int16)] * (far - 1)
    if lagged:
        outs.append(shape(info.shape))
    estimate = LONG if lagged else SHORT
    return pl.pallas_call(
        functools.partial(far_kernel, lagged=lagged, block=block, far=far),
        in_specs=[WHOLE] * 4,
        out_specs=[WHOLE] * len(outs),
        out_shape=outs,
        scratch_shapes=[
            pltpu.VMEM((far, block, half), jnp.float32),
            pltpu.VMEM((far, block, half), jnp.int16),
        ],
        compiler_params=params(),
        cost_estimate=pl.CostEstimate(flops=estimate, bytes_accessed=estimate // 1024, transcendentals=0),
        name="far_lag" if lagged else "far_zero",
    )(counts, keep, came, info)


def first_last(items):
    return [*items[1:], *items[:1]]


def last_first(items):
    return [*items[-1:], *items[:-1]]


def gathered_total(kept_ref, came_refs, rows_ref, left_ref, columns):
    block, far = kept_ref.shape[0], len(came_refs) + 1
    total = kept_ref[...]
    for index, came_ref in enumerate(came_refs):
        row = 2 * far + index
        right = rows_ref[row : row + 1, columns] * (1.0 / LEVELS**2)
        total = total + from_levels(came_ref[0:block, :]) * (left_ref[:, row : row + 1] * right)
    return total


def finish_lag_kernel(counts_ref, info_ref, kept_ref, *refs, far):
    came_refs = last_first(refs[: far - 1])
    out_ref, zero_ref, rows_ref, left_ref, turned_ref = refs[far - 1 :]
    block, half = kept_ref.shape
    columns = side_columns(half, True)
    found = [decode(came_ref[block : block + TAIL, :]) for came_ref in came_refs]
    rows = [info_ref[4:5, :]] + [f[0] for f in found] + [info_ref[5:6, :]] + [f[1] for f in found]
    rows += [f[2] for f in found]
    rows += [jnp.zeros_like(rows[0])] * (rows_ref.shape[0] - len(rows))
    rows_ref[...] = jnp.concatenate(rows, axis=0)
    turned_ref[...] = jnp.transpose(rows_ref[...])
    first = pl.multiple_of(lax.axis_index("dp") * block, block)
    left_ref[...] = turned_ref[pl.ds(first, block), :]
    pair_total = counts_ref[1:2, 0:1]
    lead_mean = lead_row = lag_row = 0.0
    for k in range(far):
        lead_mean += left_ref[:, k : k + 1]
        lead_row += rows_ref[k : k + 1, columns]
        lag_row += rows_ref[far + k : far + k + 1, columns]
    lead_mean, lead_row, lag_row = (v / pair_total for v in (lead_mean, lead_row, lag_row))
    lag = gathered_total(kept_ref, came_refs, rows_ref, left_ref, columns)
    zero = jnp.zeros_like(lag)
    for k in range(far):
        weight = live_of(counts_ref, [4 * k + i for i in range(4)])
        lead = left_ref[:, k : k + 1] - lead_mean * weight
        zero = zero + lead * (rows_ref[k : k + 1, columns] / weight - lead_row)
        lag = lag + lead * (rows_ref[far + k : far + k + 1, columns] / weight - lag_row)
    out_ref[...] = lag / pair_total
    zero_ref[...] = zero


def finish_lag(counts, info, kept, came):
    block, half = kept.shape
    feats = 2 * half
    far = len(came) + 1
    rows = round_up(3 * far - 1, 8)
    return pl.pallas_call(
        functools.partial(finish_lag_kernel, far=far),
        in_specs=[WHOLE] * (3 + len(came)),
        out_specs=[WHOLE] * 4,
        out_shape=[shape(kept.shape), shape(kept.shape), shape((rows, feats)), shape((block, rows))],
        scratch_shapes=[pltpu.VMEM((feats, rows), jnp.float32)],
        compiler_params=params(),
        name="finish_lag",
    )(counts, info, kept, *first_last(came))


def finish_zero_kernel(counts_ref, rows_ref, left_ref, between_ref, kept_ref, *refs):
    came_refs, out_ref = last_first(refs[:-1]), refs[-1]
    columns = side_columns(kept_ref.shape[1], True)
    zero = gathered_total(kept_ref, came_refs, rows_ref, left_ref, columns)
    out_ref[...] = (zero + between_ref[...]) / counts_ref[1:2, 0:1]


def finish_zero(counts, rows, left, between, kept, came):
    return pl.pallas_call(
        finish_zero_kernel,
        in_specs=[WHOLE] * (5 + len(came)),
        out_specs=WHOLE,
        out_shape=shape(kept.shape),
        compiler_params=params(),
        name="finish_zero",
    )(counts, rows, left, between, kept, *first_last(came))


def exclusive(size, distance):
    return [(i, i ^ distance) for i in range(size)]


def local(coords, lengths, atom_pairs):
    feats = atom_pairs.shape[1]
    dp = lax.axis_size("dp")
    far = dp // 2
    block = feats // dp
    home = coords.shape[0]
    depth = round_up(home - LAG, DEPTH_UNIT)
    rows = round_up(max(home, depth + LAG), FRAME_TILE)

    def swap(array, axis, distance):
        return lax.ppermute(array, axis, exclusive(lax.axis_size(axis), distance))

    coords = pltpu.with_memory_space_constraint(jnp.transpose(coords, (1, 0, 2)), pltpu.HBM)
    atom_pairs = pltpu.with_memory_space_constraint(atom_pairs, pltpu.HBM)
    lengths = pltpu.with_memory_space_constraint(lengths, pltpu.HBM)
    features, stats, sent_lag, counts = contacts_call(coords, lengths, atom_pairs, rows, depth)
    common = [counts, features, stats]
    half = feats // 2
    kept_shape = shape((feats, half))
    came_lag = swap(sent_lag, "tile", 1)
    square = shape((half, half))
    kept_other, right = part_call(
        other_lag_kernel,
        common,
        [sent_lag],
        [square, shape((depth, half), jnp.bfloat16)],
        block,
        LONG,
        "kept_lag_other",
    )
    sent_shape = shape((half + TAIL, half), jnp.int16)
    sent_lag, chip = part_call(
        near_other_kernel,
        [counts, kept_other, stats, came_lag],
        [],
        [sent_shape, shape((8, feats))],
        block,
        SHORT,
        "near_lag_other",
    )
    own_came = came_lag
    came_lag = swap(sent_lag, "dp", 1)
    (kept_own,) = part_call(
        own_lag_kernel, common + [right], [sent_lag], [square], block, SHORT, "kept_lag_own"
    )
    (keep_lag,) = part_call(
        near_own_kernel, [counts, kept_own, chip, own_came], [], [square], block, SHORT, "near_lag_own"
    )
    part_shape = shape((feats // SPLIT, half), jnp.int16)
    sent_zero = gram_call(sent_zero_kernel, common, [keep_lag], [part_shape] * SPLIT, depth, SHORT)
    (kept_zero,) = gram_call(kept_zero_kernel, common, sent_zero[:1], [kept_shape], depth, SHORT)
    came_zero = [swap(part, "tile", 1) for part in sent_zero]
    near_zero = [counts, kept_zero, chip] + came_zero
    (sent_zero,) = part_call(
        functools.partial(near_zero_kernel, own=False),
        near_zero,
        [],
        [shape((half, half), jnp.int16)],
        block,
        SHORT,
        "near_zero_other",
    )
    (keep_zero,) = part_call(
        functools.partial(near_zero_kernel, own=True), near_zero, [], [square], block, SHORT, "near_zero_own"
    )
    came_zero = swap(sent_zero, "dp", 1)

    kept_lag, *sent_lag, pair = far_call(counts, keep_lag, came_lag, chip, block, True)
    came_lag = [swap(s, "dp", 2 * (i + 1)) for i, s in enumerate(sent_lag)]
    kept_zero, *sent_zero = far_call(counts, keep_zero, came_zero, pair, block, False)
    came_zero = [swap(s, "dp", 2 * (i + 1)) for i, s in enumerate(sent_zero)]
    cov_lag, between, total_rows, total_left = finish_lag(counts, pair, kept_lag, came_lag)
    cov_zero = finish_zero(counts, total_rows, total_left, between, kept_zero, came_zero)
    return (cov_zero, cov_lag)


def solution(mesh):
    placed = (P(("groups", "dp", "tile"), None, None), P("groups"), P())
    return jax.shard_map(
        local,
        mesh=mesh,
        in_specs=placed,
        out_specs=(P(("groups", "dp"), "tile"), P(("groups", "dp"), "tile")),
        check_vma=False,
    )
```

```python
import functools

import jax
import jax.numpy as jnp
from jax import lax
from jax.experimental import pallas as pl
from jax.experimental.pallas import tpu as pltpu
from jax.sharding import PartitionSpec as P

LAG = 500
FRAME_TILE = 640
FEATURE_TILE = 256
DEPTH_UNIT = 256
SLOPE = 6.0 * 1.4426950408889634
LEVELS = 32752.0
SLACK = 2e-5
FLOOR = 1e-36
PART = 32000.0
INVERSE_LOG_TWO = 1.4426950408889634
TAIL = 16
LANES = 128
LONG = 1 << 34
SHORT = 1 << 20
SPLIT = 2
VMEM = 12 * 1024 * 1024
WHOLE = pl.BlockSpec(memory_space=pltpu.VMEM)
SCALARS = pl.BlockSpec(memory_space=pltpu.SMEM)


def round_up(value, unit):
    return -(-value // unit) * unit


def own_place():
    return lax.axis_index("dp") * lax.axis_size("tile") + lax.axis_index("tile")


def params():
    return pltpu.CompilerParams(vmem_limit_bytes=VMEM)


def shape(dims, dtype=jnp.float32):
    return jax.ShapeDtypeStruct(dims, dtype)


def to_levels(ratio):
    root = lax.rsqrt(jnp.maximum(jnp.abs(ratio), 1e-30)) * LEVELS
    return jnp.round(ratio * root).astype(jnp.int32).astype(jnp.int16)


def parts_of(block):
    return block.astype(jnp.int32).astype(jnp.float32)


def from_levels(block):
    level = parts_of(block)
    return level * jnp.abs(level)


def encode(vectors):
    half = vectors[0].shape[1] // 2
    rows, exponents = [], []
    for vector in vectors:
        top = jnp.maximum(jnp.max(vector, axis=1, keepdims=True), 1e-37)
        exponent = jnp.ceil(jnp.log(top) * INVERSE_LOG_TWO) + 1.0
        units = vector * (jnp.exp2(-exponent) * PART)
        high = jnp.floor(units)
        low = jnp.floor((units - high) * PART)
        rows += [high[:, :half], high[:, half:], low[:, :half], low[:, half:]]
        exponents.append(jnp.broadcast_to(exponent, (1, half)))
    rows = rows + exponents + exponents[:1]
    return jnp.concatenate(rows, axis=0).astype(jnp.int32).astype(jnp.int16)


def decode(block):
    parts = parts_of(block)
    vectors = []
    for index in range(3):
        first = 4 * index
        high = jnp.concatenate([parts[first : first + 1], parts[first + 1 : first + 2]], axis=1)
        low = jnp.concatenate([parts[first + 2 : first + 3], parts[first + 3 : first + 4]], axis=1)
        scale = jnp.exp2(parts[12 + index : 13 + index, 0:1]) * (1.0 / PART)
        vectors.append((high + low * (1.0 / PART)) * scale)
    return vectors


def count_pairs(lengths_ref, counts_ref):
    place = own_place()
    lane = lax.broadcasted_iota(jnp.int32, (1, counts_ref.shape[1]), 1)
    counts = jnp.zeros(lane.shape, jnp.float32)
    total = 0
    for distance in range(lengths_ref.shape[0]):
        live = lengths_ref[place ^ distance] - LAG
        counts = jnp.where(lane == distance, live.astype(jnp.float32), counts)
        total = total + live
    counts_ref[0:1, :] = counts
    counts_ref[1:8, :] = jnp.broadcast_to(total.astype(jnp.float32), (7, counts_ref.shape[1]))


def live_of(counts_ref, distances):
    return sum(counts_ref[0:1, d : d + 1] for d in distances)


def pool(info_ref, sums, spread, count, other_block, other_count):
    lead, lag, deviation = decode(other_block)
    weight = count * other_count / (count + other_count)
    lead_step = sums[0] / count - lead / other_count
    lag_step = sums[1] / count - lag / other_count
    spread = spread + deviation * deviation + weight * (lead_step * lead_step + lag_step * lag_step)
    rows = [deviation, lead_step, lag_step, spread, sums[0] + lead, sums[1] + lag]
    info_ref[...] = jnp.concatenate(rows + rows[:2], axis=0)


def pooled_code(info_ref):
    return encode([info_ref[4:5, :], info_ref[5:6, :], jnp.sqrt(info_ref[3:4, :])])


def side_columns(half, own):
    side = lax.axis_index("tile")
    return pl.ds(pl.multiple_of((side if own else 1 - side) * half, half), half)


def load_right(features_ref, right_ref, own, lagged):
    depth, half = right_ref.shape
    first = LAG if lagged else 0
    right_ref[...] = features_ref[first : first + depth, side_columns(half, own)]


def gram_rows(features_ref, right_ref, start, live):
    depth = right_ref.shape[0]
    alive = lax.broadcasted_iota(jnp.int32, (depth, 1), 0).astype(jnp.float32) < live
    left = jnp.where(alive, features_ref[0:depth, start : start + FEATURE_TILE], 0.0)
    return lax.dot_general(
        left.astype(jnp.bfloat16),
        right_ref[...],
        (((0,), (0,)), ((), ())),
        preferred_element_type=jnp.float32,
    )


def contacts_kernel(
    lengths_ref, pairs_ref, coords_ref, features_ref, stats_ref, sent_ref, counts_ref, table_ref, right_ref
):
    step = pl.program_id(0)
    atoms, feats = table_ref.shape
    tile = coords_ref.shape[1]

    @pl.when(step == 0)
    def _():
        atom_ids = lax.broadcasted_iota(jnp.int32, (atoms, feats), 0)
        first_hit = (atom_ids == pairs_ref[0:1, :]).astype(jnp.float32)
        second_hit = (atom_ids == pairs_ref[1:2, :]).astype(jnp.float32)
        table_ref[...] = (first_hit - second_hit).astype(jnp.bfloat16)
        stats_ref[...] = jnp.zeros_like(stats_ref)
        count_pairs(lengths_ref, counts_ref)

    live = lengths_ref[own_place()] - LAG
    frame = step * tile + lax.broadcasted_iota(jnp.int32, (tile, 1), 0)
    used = (frame < live) | ((frame >= LAG) & (frame < live + LAG))
    leads = (step * tile + tile <= live).astype(jnp.float32)
    target = pl.ds(pl.multiple_of(step * tile, tile), tile)
    for start in range(0, feats, FEATURE_TILE):
        columns = slice(start, start + FEATURE_TILE)
        weights = table_ref[:, columns]
        squared = None
        for axis in range(3):
            separation = jnp.dot(coords_ref[axis], weights, preferred_element_type=jnp.float32)
            square = separation * separation
            squared = square if squared is None else squared + square
        squared = jnp.maximum(squared, 1e-30)
        distance = squared * lax.rsqrt(squared)
        value = pl.reciprocal(1.0 + jnp.exp2(distance * SLOPE - SLOPE), approx=True)
        value = jnp.where(used, value, 0.0).astype(jnp.bfloat16)
        features_ref[target, columns] = value
        value = value.astype(jnp.float32)
        total = jnp.sum(value, axis=0, keepdims=True)
        stats_ref[0:1, columns] += total * leads
        stats_ref[2:3, columns] += total
        stats_ref[3:4, columns] += jnp.sum(value * value, axis=0, keepdims=True)

    @pl.when((step * tile < live) & (step * tile + tile > live))
    def _():
        value = jnp.where(frame < live, features_ref[target, :], 0.0).astype(jnp.float32)
        stats_ref[0:1, :] += jnp.sum(value, axis=0, keepdims=True)

    @pl.when(step == 0)
    def _():
        value = features_ref[0:LAG, :].astype(jnp.float32)
        stats_ref[1:2, :] = -jnp.sum(value, axis=0, keepdims=True)

    @pl.when(step == pl.num_programs(0) - 1)
    def _():
        count = live + jnp.minimum(live, LAG)
        total = stats_ref[2:3, :]
        squares = stats_ref[3:4, :]
        stats_ref[1:2, :] += total
        spread = squares - total * total / count.astype(jnp.float32)
        stats_ref[2:3, :] = jnp.maximum(spread, 0.0) + (SLACK * squares + FLOOR)
        gram_half(counts_ref, features_ref, stats_ref, [sent_ref], right_ref, False, True)
        sent_ref[feats : feats + TAIL, :] = encode(
            [stats_ref[0:1, :], stats_ref[1:2, :], jnp.sqrt(stats_ref[2:3, :])]
        )


def contacts_call(coords, lengths, atom_pairs, rows, depth):
    atoms = coords.shape[2]
    feats = atom_pairs.shape[1]
    return pl.pallas_call(
        contacts_kernel,
        grid=(rows // FRAME_TILE,),
        in_specs=[
            SCALARS,
            pl.BlockSpec((2, feats), lambda i: (0, 0)),
            pl.BlockSpec((3, FRAME_TILE, atoms), lambda i: (0, i, 0)),
        ],
        out_specs=[WHOLE] * 4,
        out_shape=[
            shape((rows, feats), jnp.bfloat16),
            shape((8, feats)),
            shape((feats + TAIL, feats // 2), jnp.int16),
            shape((8, LANES)),
        ],
        scratch_shapes=[
            pltpu.VMEM((atoms, feats), jnp.bfloat16),
            pltpu.VMEM((depth, feats // 2), jnp.bfloat16),
        ],
        compiler_params=params(),
        name="contacts_sent_lag",
    )(lengths, atom_pairs, coords)


def gram_half(counts_ref, features_ref, stats_ref, out_refs, right_ref, kept, lagged):
    half = out_refs[0].shape[1]
    feats = 2 * half
    part = feats // len(out_refs)
    load_right(features_ref, right_ref, kept, lagged)
    columns = side_columns(half, kept)
    right = 1 if lagged else 0
    left_stats = jnp.transpose(stats_ref[...])
    live = live_of(counts_ref, [0])
    right_mean = stats_ref[right : right + 1, columns] / live
    right_inverse = lax.rsqrt(stats_ref[2:3, columns])
    for start in range(0, feats, FEATURE_TILE):
        rows = slice(start, start + FEATURE_TILE)
        gram = gram_rows(features_ref, right_ref, start, live)
        gram = gram - left_stats[rows, 0:1] * right_mean
        if not kept:
            scale = lax.rsqrt(left_stats[rows, 2:3]) * right_inverse
            gram = to_levels(gram * scale)
        first = start % part
        out_refs[start // part][first : first + FEATURE_TILE, :] = gram


def chosen(own, even, odd):
    near = lax.axis_index("dp") % 2
    return jnp.where(near == 0, even, odd) if own else jnp.where(near == 0, odd, even)


def chosen_block(own, ref, index, block):
    first = 2 * index * block
    return chosen(own, ref[first : first + block, :], ref[first + block : first + 2 * block, :])


def kept_part(counts_ref, features_ref, stats_ref, right_ref, kept_ref, own, block):
    depth, half = right_ref.shape
    columns = side_columns(half, True)
    live = live_of(counts_ref, [0])
    left_total = jnp.transpose(stats_ref[...])[:, 0:1]
    right_mean = stats_ref[1:2, columns] / live
    alive = lax.broadcasted_iota(jnp.int32, (depth, 1), 0).astype(jnp.float32) < live
    for start in range(0, half, FEATURE_TILE):
        left, totals = [], []
        for first in range(2 * start, 2 * (start + FEATURE_TILE), 2 * block):
            even, odd = slice(first, first + block), slice(first + block, first + 2 * block)
            left.append(chosen(own, features_ref[0:depth, even], features_ref[0:depth, odd]))
            totals.append(chosen(own, left_total[even], left_total[odd]))
        left = jnp.where(alive, jnp.concatenate(left, axis=1), 0.0).astype(jnp.bfloat16)
        gram = lax.dot_general(
            left, right_ref[...], (((0,), (0,)), ((), ())), preferred_element_type=jnp.float32
        )
        total = jnp.concatenate(totals, axis=0)
        kept_ref[start : start + FEATURE_TILE, :] = gram - total * right_mean


def other_lag_kernel(counts_ref, features_ref, stats_ref, _, kept_ref, right_ref, *, block):
    load_right(features_ref, right_ref, True, True)
    kept_part(counts_ref, features_ref, stats_ref, right_ref, kept_ref, False, block)


def own_lag_kernel(counts_ref, features_ref, stats_ref, right_ref, _, kept_ref, *, block):
    kept_part(counts_ref, features_ref, stats_ref, right_ref, kept_ref, True, block)


def part_call(body, operands, after, outs, block, estimate, name):
    return pl.pallas_call(
        functools.partial(body, block=block),
        in_specs=[WHOLE] * len(operands) + [pl.BlockSpec(memory_space=pl.ANY)] * len(after),
        out_specs=[WHOLE] * len(outs),
        out_shape=outs,
        compiler_params=params(),
        cost_estimate=pl.CostEstimate(flops=estimate, bytes_accessed=estimate // 1024, transcendentals=0),
        name=name,
    )(*operands, *after)


def near_other_kernel(counts_ref, kept_ref, stats_ref, came_ref, sent_ref, info_ref, *, block):
    half = kept_ref.shape[0]
    feats = 2 * half
    columns = side_columns(half, True)
    count, peer_count = live_of(counts_ref, [0]), live_of(counts_ref, [1])
    sums = (stats_ref[0:1, :], stats_ref[1:2, :])
    pool(info_ref, sums, stats_ref[2:3, :], count, came_ref[feats : feats + TAIL, :], peer_count)
    sent_ref[half : half + TAIL, :] = pooled_code(info_ref)
    weight = count * peer_count / (count + peer_count)
    left = jnp.transpose(info_ref[...])
    came_right = info_ref[0:1, columns] * (1.0 / LEVELS**2)
    step_right = info_ref[2:3, columns] * weight
    sent_right = lax.rsqrt(info_ref[3:4, columns])
    for index in range(half // block):
        rows = slice(index * block, (index + 1) * block)
        mine = chosen_block(False, left, index, block)
        came = from_levels(chosen_block(False, came_ref, index, block))
        total = kept_ref[rows, :] + came * (mine[:, 0:1] * came_right) + mine[:, 1:2] * step_right
        sent_ref[rows, :] = to_levels(total * (lax.rsqrt(mine[:, 3:4]) * sent_right))


def near_own_kernel(counts_ref, kept_ref, info_ref, came_ref, keep_ref, *, block):
    half = kept_ref.shape[0]
    columns = side_columns(half, True)
    count, peer_count = live_of(counts_ref, [0]), live_of(counts_ref, [1])
    weight = count * peer_count / (count + peer_count)
    left = jnp.transpose(info_ref[...])
    came_right = info_ref[0:1, columns] * (1.0 / LEVELS**2)
    step_right = info_ref[2:3, columns] * weight
    for index in range(half // block):
        rows = slice(index * block, (index + 1) * block)
        mine = chosen_block(True, left, index, block)
        came = from_levels(chosen_block(True, came_ref, index, block))
        keep_ref[rows, :] = (
            kept_ref[rows, :] + came * (mine[:, 0:1] * came_right) + mine[:, 1:2] * step_right
        )


def sent_zero_kernel(counts_ref, features_ref, stats_ref, _, *refs):
    gram_half(counts_ref, features_ref, stats_ref, refs[:-1], refs[-1], False, False)


def kept_zero_kernel(counts_ref, features_ref, stats_ref, _, kept_ref, right_ref):
    gram_half(counts_ref, features_ref, stats_ref, [kept_ref], right_ref, True, False)


def gram_call(body, operands, after, outs, depth, estimate):
    feats = operands[1].shape[1]
    return pl.pallas_call(
        body,
        in_specs=[WHOLE] * len(operands)
        + [pl.BlockSpec(memory_space=pl.ANY)] * len(after),
        out_specs=[WHOLE] * len(outs),
        out_shape=outs,
        scratch_shapes=[pltpu.VMEM((depth, feats // 2), jnp.bfloat16)],
        compiler_params=params(),
        cost_estimate=pl.CostEstimate(flops=estimate, bytes_accessed=estimate // 1024, transcendentals=0),
        name=body.__name__.removesuffix("_kernel"),
    )(*operands, *after)


def near_zero_kernel(counts_ref, kept_ref, info_ref, *refs, own, block):
    came_refs, out_ref = refs[:-1], refs[-1]
    feats, half = kept_ref.shape
    part = feats // len(came_refs)
    columns = side_columns(half, True)
    count, peer_count = live_of(counts_ref, [0]), live_of(counts_ref, [1])
    weight = count * peer_count / (count + peer_count)
    left = jnp.transpose(info_ref[...])
    came_right = info_ref[0:1, columns] * (1.0 / LEVELS**2)
    step_right = info_ref[1:2, columns] * weight
    sent_right = lax.rsqrt(info_ref[3:4, columns])
    for index in range(half // block):
        mine = chosen_block(own, left, index, block)
        kept = chosen_block(own, kept_ref, index, block)
        came_ref, inside = came_refs[2 * index * block // part], 2 * index * block % part
        even, odd = came_ref[inside : inside + block, :], came_ref[inside + block : inside + 2 * block, :]
        came = from_levels(chosen(own, even, odd))
        total = kept + came * (mine[:, 0:1] * came_right) + mine[:, 1:2] * step_right
        if not own:
            total = to_levels(total * (lax.rsqrt(mine[:, 3:4]) * sent_right))
        out_ref[index * block : (index + 1) * block, :] = total


def far_kernel(counts_ref, keep_ref, came_ref, info_ref, *refs, lagged, block, far):
    kept_ref, sent_refs = refs[0], refs[1:far]
    total_ref, level_ref = refs[-2], refs[-1]
    place = lax.axis_index("dp")
    near, own_far = place % 2, place // 2
    half = keep_ref.shape[0]
    columns = side_columns(half, True)
    count, near_count = live_of(counts_ref, [0, 1]), live_of(counts_ref, [2, 3])
    if lagged:
        chip_ref, info_ref = info_ref, refs[far]
        sums = (chip_ref[4:5, :], chip_ref[5:6, :])
        pool(info_ref, sums, chip_ref[3:4, :], count, came_ref[half : half + TAIL, :], near_count)
        code = pooled_code(info_ref)
        for sent_ref in sent_refs:
            sent_ref[block : block + TAIL, :] = code
    weight = count * near_count / (count + near_count)
    left = jnp.transpose(info_ref[...])
    came_right = info_ref[0:1, columns] * (1.0 / LEVELS**2)
    step_right = info_ref[2 if lagged else 1 : 3 if lagged else 2, columns] * weight
    sent_right = lax.rsqrt(info_ref[3:4, columns])
    for index in range(far):
        rows = slice(index * block, (index + 1) * block)
        even = left[2 * index * block : (2 * index + 1) * block]
        odd = left[(2 * index + 1) * block : (2 * index + 2) * block]
        mine = jnp.where(near == 0, even, odd)
        total = keep_ref[rows, :] + from_levels(came_ref[rows, :]) * (mine[:, 0:1] * came_right)
        total = total + mine[:, 1:2] * step_right
        total_ref[index] = total
        level_ref[index] = to_levels(total * (lax.rsqrt(mine[:, 3:4]) * sent_right))
    kept_ref[...] = total_ref[own_far]
    for step, sent_ref in enumerate(sent_refs):
        sent_ref[0:block, :] = level_ref[own_far ^ (step + 1)]


def far_call(counts, keep, came, info, block, lagged):
    half = keep.shape[0]
    far = half // block
    outs = [shape((block, half))]
    outs += [shape((block + (TAIL if lagged else 0), half), jnp.int16)] * (far - 1)
    if lagged:
        outs.append(shape(info.shape))
    estimate = LONG if lagged else SHORT
    return pl.pallas_call(
        functools.partial(far_kernel, lagged=lagged, block=block, far=far),
        in_specs=[WHOLE] * 4,
        out_specs=[WHOLE] * len(outs),
        out_shape=outs,
        scratch_shapes=[
            pltpu.VMEM((far, block, half), jnp.float32),
            pltpu.VMEM((far, block, half), jnp.int16),
        ],
        compiler_params=params(),
        cost_estimate=pl.CostEstimate(flops=estimate, bytes_accessed=estimate // 1024, transcendentals=0),
        name="far_lag" if lagged else "far_zero",
    )(counts, keep, came, info)


def first_last(items):
    return [*items[1:], *items[:1]]


def last_first(items):
    return [*items[-1:], *items[:-1]]


def gathered_total(kept_ref, came_refs, rows_ref, left_ref, columns):
    block, far = kept_ref.shape[0], len(came_refs) + 1
    total = kept_ref[...]
    for index, came_ref in enumerate(came_refs):
        row = 2 * far + index
        right = rows_ref[row : row + 1, columns] * (1.0 / LEVELS**2)
        total = total + from_levels(came_ref[0:block, :]) * (left_ref[:, row : row + 1] * right)
    return total


def finish_lag_kernel(counts_ref, info_ref, kept_ref, *refs, far):
    came_refs = last_first(refs[: far - 1])
    out_ref, zero_ref, rows_ref, left_ref, turned_ref = refs[far - 1 :]
    block, half = kept_ref.shape
    columns = side_columns(half, True)
    found = [decode(came_ref[block : block + TAIL, :]) for came_ref in came_refs]
    rows = [info_ref[4:5, :]] + [f[0] for f in found] + [info_ref[5:6, :]] + [f[1] for f in found]
    rows += [f[2] for f in found]
    rows += [jnp.zeros_like(rows[0])] * (rows_ref.shape[0] - len(rows))
    rows_ref[...] = jnp.concatenate(rows, axis=0)
    turned_ref[...] = jnp.transpose(rows_ref[...])
    first = pl.multiple_of(lax.axis_index("dp") * block, block)
    left_ref[...] = turned_ref[pl.ds(first, block), :]
    pair_total = counts_ref[1:2, 0:1]
    lead_mean = lead_row = lag_row = 0.0
    for k in range(far):
        lead_mean += left_ref[:, k : k + 1]
        lead_row += rows_ref[k : k + 1, columns]
        lag_row += rows_ref[far + k : far + k + 1, columns]
    lead_mean, lead_row, lag_row = (v / pair_total for v in (lead_mean, lead_row, lag_row))
    lag = gathered_total(kept_ref, came_refs, rows_ref, left_ref, columns)
    zero = jnp.zeros_like(lag)
    for k in range(far):
        weight = live_of(counts_ref, [4 * k + i for i in range(4)])
        lead = left_ref[:, k : k + 1] - lead_mean * weight
        zero = zero + lead * (rows_ref[k : k + 1, columns] / weight - lead_row)
        lag = lag + lead * (rows_ref[far + k : far + k + 1, columns] / weight - lag_row)
    out_ref[...] = lag / pair_total
    zero_ref[...] = zero


def finish_lag(counts, info, kept, came):
    block, half = kept.shape
    feats = 2 * half
    far = len(came) + 1
    rows = round_up(3 * far - 1, 8)
    return pl.pallas_call(
        functools.partial(finish_lag_kernel, far=far),
        in_specs=[WHOLE] * (3 + len(came)),
        out_specs=[WHOLE] * 4,
        out_shape=[shape(kept.shape), shape(kept.shape), shape((rows, feats)), shape((block, rows))],
        scratch_shapes=[pltpu.VMEM((feats, rows), jnp.float32)],
        compiler_params=params(),
        name="finish_lag",
    )(counts, info, kept, *first_last(came))


def finish_zero_kernel(counts_ref, rows_ref, left_ref, between_ref, kept_ref, *refs):
    came_refs, out_ref = last_first(refs[:-1]), refs[-1]
    columns = side_columns(kept_ref.shape[1], True)
    zero = gathered_total(kept_ref, came_refs, rows_ref, left_ref, columns)
    out_ref[...] = (zero + between_ref[...]) / counts_ref[1:2, 0:1]


def finish_zero(counts, rows, left, between, kept, came):
    return pl.pallas_call(
        finish_zero_kernel,
        in_specs=[WHOLE] * (5 + len(came)),
        out_specs=WHOLE,
        out_shape=shape(kept.shape),
        compiler_params=params(),
        name="finish_zero",
    )(counts, rows, left, between, kept, *first_last(came))


def exclusive(size, distance):
    return [(i, i ^ distance) for i in range(size)]


def local(coords, lengths, atom_pairs):
    feats = atom_pairs.shape[1]
    dp = lax.axis_size("dp")
    far = dp // 2
    block = feats // dp
    home = coords.shape[0]
    depth = round_up(home - LAG, DEPTH_UNIT)
    rows = round_up(max(home, depth + LAG), FRAME_TILE)

    def swap(array, axis, distance):
        return lax.ppermute(array, axis, exclusive(lax.axis_size(axis), distance))

    coords = pltpu.with_memory_space_constraint(jnp.transpose(coords, (1, 0, 2)), pltpu.HBM)
    atom_pairs = pltpu.with_memory_space_constraint(atom_pairs, pltpu.HBM)
    lengths = pltpu.with_memory_space_constraint(lengths, pltpu.HBM)
    features, stats, sent_lag, counts = contacts_call(coords, lengths, atom_pairs, rows, depth)
    common = [counts, features, stats]
    half = feats // 2
    kept_shape = shape((feats, half))
    came_lag = swap(sent_lag, "tile", 1)
    square = shape((half, half))
    kept_other, right = part_call(
        other_lag_kernel,
        common,
        [sent_lag],
        [square, shape((depth, half), jnp.bfloat16)],
        block,
        LONG,
        "kept_lag_other",
    )
    sent_shape = shape((half + TAIL, half), jnp.int16)
    sent_lag, chip = part_call(
        near_other_kernel,
        [counts, kept_other, stats, came_lag],
        [],
        [sent_shape, shape((8, feats))],
        block,
        SHORT,
        "near_lag_other",
    )
    own_came = came_lag
    came_lag = swap(sent_lag, "dp", 1)
    (kept_own,) = part_call(
        own_lag_kernel, common + [right], [sent_lag], [square], block, SHORT, "kept_lag_own"
    )
    (keep_lag,) = part_call(
        near_own_kernel, [counts, kept_own, chip, own_came], [], [square], block, SHORT, "near_lag_own"
    )
    part_shape = shape((feats // SPLIT, half), jnp.int16)
    sent_zero = gram_call(sent_zero_kernel, common, [keep_lag], [part_shape] * SPLIT, depth, SHORT)
    (kept_zero,) = gram_call(kept_zero_kernel, common, sent_zero[:1], [kept_shape], depth, SHORT)
    came_zero = [swap(part, "tile", 1) for part in sent_zero]
    near_zero = [counts, kept_zero, chip] + came_zero
    (sent_zero,) = part_call(
        functools.partial(near_zero_kernel, own=False),
        near_zero,
        [],
        [shape((half, half), jnp.int16)],
        block,
        SHORT,
        "near_zero_other",
    )
    (keep_zero,) = part_call(
        functools.partial(near_zero_kernel, own=True), near_zero, [], [square], block, SHORT, "near_zero_own"
    )
    came_zero = swap(sent_zero, "dp", 1)

    kept_lag, *sent_lag, pair = far_call(counts, keep_lag, came_lag, chip, block, True)
    came_lag = [swap(s, "dp", 2 * (i + 1)) for i, s in enumerate(sent_lag)]
    kept_zero, *sent_zero = far_call(counts, keep_zero, came_zero, pair, block, False)
    came_zero = [swap(s, "dp", 2 * (i + 1)) for i, s in enumerate(sent_zero)]
    cov_lag, between, total_rows, total_left = finish_lag(counts, pair, kept_lag, came_lag)
    cov_zero = finish_zero(counts, total_rows, total_left, between, kept_zero, came_zero)
    return (cov_zero, cov_lag)


def solution(mesh):
    placed = (P(("groups", "dp", "tile"), None, None), P("groups"), P())
    return jax.shard_map(
        local,
        mesh=mesh,
        in_specs=placed,
        out_specs=(P(("groups", "dp"), "tile"), P(("groups", "dp"), "tile")),
        check_vma=False,
    )
```

```python
import functools

import jax
import jax.numpy as jnp
from jax import lax
from jax.experimental import pallas as pl
from jax.experimental.pallas import tpu as pltpu
from jax.sharding import PartitionSpec as P

LAG = 500
FRAME_TILE = 640
FEATURE_TILE = 256
DEPTH_UNIT = 256
SLOPE = 6.0 * 1.4426950408889634
LEVELS = 32752.0
SLACK = 2e-5
FLOOR = 1e-36
PART = 32000.0
INVERSE_LOG_TWO = 1.4426950408889634
TAIL = 16
LANES = 128
LONG = 1 << 34
SHORT = 1 << 20
SPLIT = 2
VMEM = 12 * 1024 * 1024
CONTACTS_VMEM = 20 * 1024 * 1024
WHOLE = pl.BlockSpec(memory_space=pltpu.VMEM)
SCALARS = pl.BlockSpec(memory_space=pltpu.SMEM)


def round_up(value, unit):
    return -(-value // unit) * unit


def own_place():
    return lax.axis_index("dp") * lax.axis_size("tile") + lax.axis_index("tile")


def params():
    return pltpu.CompilerParams(vmem_limit_bytes=VMEM)


def shape(dims, dtype=jnp.float32):
    return jax.ShapeDtypeStruct(dims, dtype)


def to_levels(ratio):
    root = lax.rsqrt(jnp.maximum(jnp.abs(ratio), 1e-30)) * LEVELS
    return jnp.round(ratio * root).astype(jnp.int32).astype(jnp.int16)


def parts_of(block):
    return block.astype(jnp.int32).astype(jnp.float32)


def from_levels(block):
    level = parts_of(block)
    return level * jnp.abs(level)


def encode(vectors):
    half = vectors[0].shape[1] // 2
    rows, exponents = [], []
    for vector in vectors:
        top = jnp.maximum(jnp.max(vector, axis=1, keepdims=True), 1e-37)
        exponent = jnp.ceil(jnp.log(top) * INVERSE_LOG_TWO) + 1.0
        units = vector * (jnp.exp2(-exponent) * PART)
        high = jnp.floor(units)
        low = jnp.floor((units - high) * PART)
        rows += [high[:, :half], high[:, half:], low[:, :half], low[:, half:]]
        exponents.append(jnp.broadcast_to(exponent, (1, half)))
    rows = rows + exponents + exponents[:1]
    return jnp.concatenate(rows, axis=0).astype(jnp.int32).astype(jnp.int16)


def decode(block):
    parts = parts_of(block)
    vectors = []
    for index in range(3):
        first = 4 * index
        high = jnp.concatenate([parts[first : first + 1], parts[first + 1 : first + 2]], axis=1)
        low = jnp.concatenate([parts[first + 2 : first + 3], parts[first + 3 : first + 4]], axis=1)
        scale = jnp.exp2(parts[12 + index : 13 + index, 0:1]) * (1.0 / PART)
        vectors.append((high + low * (1.0 / PART)) * scale)
    return vectors


def count_pairs(lengths_ref, counts_ref):
    place = own_place()
    lane = lax.broadcasted_iota(jnp.int32, (1, counts_ref.shape[1]), 1)
    counts = jnp.zeros(lane.shape, jnp.float32)
    total = 0
    for distance in range(lengths_ref.shape[0]):
        live = lengths_ref[place ^ distance] - LAG
        counts = jnp.where(lane == distance, live.astype(jnp.float32), counts)
        total = total + live
    counts_ref[0:1, :] = counts
    counts_ref[1:8, :] = jnp.broadcast_to(total.astype(jnp.float32), (7, counts_ref.shape[1]))


def live_of(counts_ref, distances):
    return sum(counts_ref[0:1, d : d + 1] for d in distances)


def pool(info_ref, sums, spread, count, other_block, other_count):
    lead, lag, deviation = decode(other_block)
    weight = count * other_count / (count + other_count)
    lead_step = sums[0] / count - lead / other_count
    lag_step = sums[1] / count - lag / other_count
    spread = spread + deviation * deviation + weight * (lead_step * lead_step + lag_step * lag_step)
    rows = [deviation, lead_step, lag_step, spread, sums[0] + lead, sums[1] + lag]
    info_ref[...] = jnp.concatenate(rows + rows[:2], axis=0)


def pooled_code(info_ref):
    return encode([info_ref[4:5, :], info_ref[5:6, :], jnp.sqrt(info_ref[3:4, :])])


def side_columns(half, own):
    side = lax.axis_index("tile")
    return pl.ds(pl.multiple_of((side if own else 1 - side) * half, half), half)


def load_right(features_ref, right_ref, own, lagged):
    depth, half = right_ref.shape
    first = LAG if lagged else 0
    right_ref[...] = features_ref[first : first + depth, side_columns(half, own)]


def gram_rows(features_ref, right_ref, start, live):
    depth = right_ref.shape[0]
    alive = lax.broadcasted_iota(jnp.int32, (depth, 1), 0).astype(jnp.float32) < live
    left = jnp.where(alive, features_ref[0:depth, start : start + FEATURE_TILE], 0.0)
    return lax.dot_general(
        left.astype(jnp.bfloat16),
        right_ref[...],
        (((0,), (0,)), ((), ())),
        preferred_element_type=jnp.float32,
    )


def contacts_chunk(step, live, frames_ref, table_ref, features_ref, stats_ref):
    tile = frames_ref.shape[2]
    feats = table_ref.shape[1]
    frame = step * tile + lax.broadcasted_iota(jnp.int32, (tile, 1), 0)
    used = (frame < live) | ((frame >= LAG) & (frame < live + LAG))
    leads = (step * tile + tile <= live).astype(jnp.float32)
    target = pl.ds(pl.multiple_of(step * tile, tile), tile)
    for start in range(0, feats, FEATURE_TILE):
        columns = slice(start, start + FEATURE_TILE)
        weights = table_ref[:, columns]
        squared = None
        for axis in range(3):
            separation = jnp.dot(frames_ref[step, axis], weights, preferred_element_type=jnp.float32)
            square = separation * separation
            squared = square if squared is None else squared + square
        squared = jnp.maximum(squared, 1e-30)
        distance = squared * lax.rsqrt(squared)
        value = pl.reciprocal(1.0 + jnp.exp2(distance * SLOPE - SLOPE), approx=True)
        value = jnp.where(used, value, 0.0).astype(jnp.bfloat16)
        features_ref[target, columns] = value
        value = value.astype(jnp.float32)
        total = jnp.sum(value, axis=0, keepdims=True)
        stats_ref[0:1, columns] += total * leads
        stats_ref[2:3, columns] += total
        stats_ref[3:4, columns] += jnp.sum(value * value, axis=0, keepdims=True)

    @pl.when((step * tile < live) & (step * tile + tile > live))
    def _():
        value = jnp.where(frame < live, features_ref[target, :], 0.0).astype(jnp.float32)
        stats_ref[0:1, :] += jnp.sum(value, axis=0, keepdims=True)


def contacts_kernel(
    lengths_ref, pairs_ref, coords_ref, tail_ref, features_ref, stats_ref, sent_ref, counts_ref,
    table_ref, right_ref, frames_ref, arrived
):
    atoms, feats = table_ref.shape
    chunks, _, tile, _ = frames_ref.shape
    whole = chunks - 1

    def chunk_copy(step):
        rows = pl.ds(pl.multiple_of(step * tile, tile), tile)
        return pltpu.make_async_copy(coords_ref.at[:, rows, :], frames_ref.at[step], arrived.at[step])

    for step in range(whole):
        chunk_copy(step).start()
    atom_ids = lax.broadcasted_iota(jnp.int32, (atoms, feats), 0)
    first_hit = (atom_ids == pairs_ref[0:1, :]).astype(jnp.float32)
    second_hit = (atom_ids == pairs_ref[1:2, :]).astype(jnp.float32)
    table_ref[...] = (first_hit - second_hit).astype(jnp.bfloat16)
    stats_ref[...] = jnp.zeros_like(stats_ref)
    count_pairs(lengths_ref, counts_ref)
    frames_ref[whole] = tail_ref[...]
    live = lengths_ref[own_place()] - LAG

    def one_chunk(index, carry):
        step = lax.rem(index + whole, chunks)

        @pl.when(index > 0)
        def _():
            chunk_copy(step).wait()

        contacts_chunk(step, live, frames_ref, table_ref, features_ref, stats_ref)
        return carry

    lax.fori_loop(0, chunks, one_chunk, 0)
    head = jnp.sum(features_ref[0:LAG, :].astype(jnp.float32), axis=0, keepdims=True)
    count = live + jnp.minimum(live, LAG)
    total = stats_ref[2:3, :]
    squares = stats_ref[3:4, :]
    stats_ref[1:2, :] = total - head
    spread = squares - total * total / count.astype(jnp.float32)
    stats_ref[2:3, :] = jnp.maximum(spread, 0.0) + (SLACK * squares + FLOOR)
    gram_half(counts_ref, features_ref, stats_ref, [sent_ref], right_ref, False, True)
    sent_ref[feats : feats + TAIL, :] = encode(
        [stats_ref[0:1, :], stats_ref[1:2, :], jnp.sqrt(stats_ref[2:3, :])]
    )


def contacts_call(coords, lengths, atom_pairs, rows, depth):
    atoms = coords.shape[2]
    feats = atom_pairs.shape[1]
    chunks = rows // FRAME_TILE
    assert (chunks - 1) * FRAME_TILE < coords.shape[1] <= rows
    return pl.pallas_call(
        contacts_kernel,
        grid=(1,),
        in_specs=[
            SCALARS,
            pl.BlockSpec((2, feats), lambda i: (0, 0)),
            pl.BlockSpec(memory_space=pl.ANY),
            pl.BlockSpec((3, FRAME_TILE, atoms), lambda i: (0, chunks - 1, 0)),
        ],
        out_specs=[WHOLE] * 4,
        out_shape=[
            shape((rows, feats), jnp.bfloat16),
            shape((8, feats)),
            shape((feats + TAIL, feats // 2), jnp.int16),
            shape((8, LANES)),
        ],
        scratch_shapes=[
            pltpu.VMEM((atoms, feats), jnp.bfloat16),
            pltpu.VMEM((depth, feats // 2), jnp.bfloat16),
            pltpu.VMEM((chunks, 3, FRAME_TILE, atoms), jnp.bfloat16),
            pltpu.SemaphoreType.DMA((chunks,)),
        ],
        compiler_params=pltpu.CompilerParams(vmem_limit_bytes=CONTACTS_VMEM),
        name="contacts_sent_lag",
    )(lengths, atom_pairs, coords, coords)


def gram_half(counts_ref, features_ref, stats_ref, out_refs, right_ref, kept, lagged):
    half = out_refs[0].shape[1]
    feats = 2 * half
    part = feats // len(out_refs)
    load_right(features_ref, right_ref, kept, lagged)
    columns = side_columns(half, kept)
    right = 1 if lagged else 0
    left_stats = jnp.transpose(stats_ref[...])
    live = live_of(counts_ref, [0])
    right_mean = stats_ref[right : right + 1, columns] / live
    right_inverse = lax.rsqrt(stats_ref[2:3, columns])
    for start in range(0, feats, FEATURE_TILE):
        rows = slice(start, start + FEATURE_TILE)
        gram = gram_rows(features_ref, right_ref, start, live)
        gram = gram - left_stats[rows, 0:1] * right_mean
        if not kept:
            scale = lax.rsqrt(left_stats[rows, 2:3]) * right_inverse
            gram = to_levels(gram * scale)
        first = start % part
        out_refs[start // part][first : first + FEATURE_TILE, :] = gram


def chosen(own, even, odd):
    near = lax.axis_index("dp") % 2
    return jnp.where(near == 0, even, odd) if own else jnp.where(near == 0, odd, even)


def chosen_block(own, ref, index, block):
    first = 2 * index * block
    return chosen(own, ref[first : first + block, :], ref[first + block : first + 2 * block, :])


def kept_part(counts_ref, features_ref, stats_ref, right_ref, kept_ref, own, block):
    depth, half = right_ref.shape
    columns = side_columns(half, True)
    live = live_of(counts_ref, [0])
    left_total = jnp.transpose(stats_ref[...])[:, 0:1]
    right_mean = stats_ref[1:2, columns] / live
    alive = lax.broadcasted_iota(jnp.int32, (depth, 1), 0).astype(jnp.float32) < live
    for start in range(0, half, FEATURE_TILE):
        left, totals = [], []
        for first in range(2 * start, 2 * (start + FEATURE_TILE), 2 * block):
            even, odd = slice(first, first + block), slice(first + block, first + 2 * block)
            left.append(chosen(own, features_ref[0:depth, even], features_ref[0:depth, odd]))
            totals.append(chosen(own, left_total[even], left_total[odd]))
        left = jnp.where(alive, jnp.concatenate(left, axis=1), 0.0).astype(jnp.bfloat16)
        gram = lax.dot_general(
            left, right_ref[...], (((0,), (0,)), ((), ())), preferred_element_type=jnp.float32
        )
        total = jnp.concatenate(totals, axis=0)
        kept_ref[start : start + FEATURE_TILE, :] = gram - total * right_mean


def other_lag_kernel(counts_ref, features_ref, stats_ref, _, kept_ref, right_ref, *, block):
    load_right(features_ref, right_ref, True, True)
    kept_part(counts_ref, features_ref, stats_ref, right_ref, kept_ref, False, block)


def own_lag_kernel(counts_ref, features_ref, stats_ref, right_ref, _, kept_ref, *, block):
    kept_part(counts_ref, features_ref, stats_ref, right_ref, kept_ref, True, block)


def part_call(body, operands, after, outs, block, estimate, name):
    return pl.pallas_call(
        functools.partial(body, block=block),
        in_specs=[WHOLE] * len(operands) + [pl.BlockSpec(memory_space=pl.ANY)] * len(after),
        out_specs=[WHOLE] * len(outs),
        out_shape=outs,
        compiler_params=params(),
        cost_estimate=pl.CostEstimate(flops=estimate, bytes_accessed=estimate // 1024, transcendentals=0),
        name=name,
    )(*operands, *after)


def near_other_kernel(counts_ref, kept_ref, stats_ref, came_ref, sent_ref, info_ref, *, block):
    half = kept_ref.shape[0]
    feats = 2 * half
    columns = side_columns(half, True)
    count, peer_count = live_of(counts_ref, [0]), live_of(counts_ref, [1])
    sums = (stats_ref[0:1, :], stats_ref[1:2, :])
    pool(info_ref, sums, stats_ref[2:3, :], count, came_ref[feats : feats + TAIL, :], peer_count)
    sent_ref[half : half + TAIL, :] = pooled_code(info_ref)
    weight = count * peer_count / (count + peer_count)
    left = jnp.transpose(info_ref[...])
    came_right = info_ref[0:1, columns] * (1.0 / LEVELS**2)
    step_right = info_ref[2:3, columns] * weight
    sent_right = lax.rsqrt(info_ref[3:4, columns])
    for index in range(half // block):
        rows = slice(index * block, (index + 1) * block)
        mine = chosen_block(False, left, index, block)
        came = from_levels(chosen_block(False, came_ref, index, block))
        total = kept_ref[rows, :] + came * (mine[:, 0:1] * came_right) + mine[:, 1:2] * step_right
        sent_ref[rows, :] = to_levels(total * (lax.rsqrt(mine[:, 3:4]) * sent_right))


def near_own_kernel(counts_ref, kept_ref, info_ref, came_ref, keep_ref, *, block):
    half = kept_ref.shape[0]
    columns = side_columns(half, True)
    count, peer_count = live_of(counts_ref, [0]), live_of(counts_ref, [1])
    weight = count * peer_count / (count + peer_count)
    left = jnp.transpose(info_ref[...])
    came_right = info_ref[0:1, columns] * (1.0 / LEVELS**2)
    step_right = info_ref[2:3, columns] * weight
    for index in range(half // block):
        rows = slice(index * block, (index + 1) * block)
        mine = chosen_block(True, left, index, block)
        came = from_levels(chosen_block(True, came_ref, index, block))
        keep_ref[rows, :] = (
            kept_ref[rows, :] + came * (mine[:, 0:1] * came_right) + mine[:, 1:2] * step_right
        )


def sent_zero_kernel(counts_ref, features_ref, stats_ref, _, *refs):
    gram_half(counts_ref, features_ref, stats_ref, refs[:-1], refs[-1], False, False)


def kept_zero_kernel(counts_ref, features_ref, stats_ref, _, kept_ref, right_ref):
    gram_half(counts_ref, features_ref, stats_ref, [kept_ref], right_ref, True, False)


def gram_call(body, operands, after, outs, depth, estimate):
    feats = operands[1].shape[1]
    return pl.pallas_call(
        body,
        in_specs=[WHOLE] * len(operands)
        + [pl.BlockSpec(memory_space=pl.ANY)] * len(after),
        out_specs=[WHOLE] * len(outs),
        out_shape=outs,
        scratch_shapes=[pltpu.VMEM((depth, feats // 2), jnp.bfloat16)],
        compiler_params=params(),
        cost_estimate=pl.CostEstimate(flops=estimate, bytes_accessed=estimate // 1024, transcendentals=0),
        name=body.__name__.removesuffix("_kernel"),
    )(*operands, *after)


def near_zero_kernel(counts_ref, kept_ref, info_ref, *refs, own, block):
    came_refs, out_ref = refs[:-1], refs[-1]
    feats, half = kept_ref.shape
    part = feats // len(came_refs)
    columns = side_columns(half, True)
    count, peer_count = live_of(counts_ref, [0]), live_of(counts_ref, [1])
    weight = count * peer_count / (count + peer_count)
    left = jnp.transpose(info_ref[...])
    came_right = info_ref[0:1, columns] * (1.0 / LEVELS**2)
    step_right = info_ref[1:2, columns] * weight
    sent_right = lax.rsqrt(info_ref[3:4, columns])
    for index in range(half // block):
        mine = chosen_block(own, left, index, block)
        kept = chosen_block(own, kept_ref, index, block)
        came_ref, inside = came_refs[2 * index * block // part], 2 * index * block % part
        even, odd = came_ref[inside : inside + block, :], came_ref[inside + block : inside + 2 * block, :]
        came = from_levels(chosen(own, even, odd))
        total = kept + came * (mine[:, 0:1] * came_right) + mine[:, 1:2] * step_right
        if not own:
            total = to_levels(total * (lax.rsqrt(mine[:, 3:4]) * sent_right))
        out_ref[index * block : (index + 1) * block, :] = total


def far_kernel(counts_ref, keep_ref, came_ref, info_ref, *refs, lagged, block, far):
    kept_ref, sent_refs = refs[0], refs[1:far]
    total_ref, level_ref = refs[-2], refs[-1]
    place = lax.axis_index("dp")
    near, own_far = place % 2, place // 2
    half = keep_ref.shape[0]
    columns = side_columns(half, True)
    count, near_count = live_of(counts_ref, [0, 1]), live_of(counts_ref, [2, 3])
    if lagged:
        chip_ref, info_ref = info_ref, refs[far]
        sums = (chip_ref[4:5, :], chip_ref[5:6, :])
        pool(info_ref, sums, chip_ref[3:4, :], count, came_ref[half : half + TAIL, :], near_count)
        code = pooled_code(info_ref)
        for sent_ref in sent_refs:
            sent_ref[block : block + TAIL, :] = code
    weight = count * near_count / (count + near_count)
    left = jnp.transpose(info_ref[...])
    came_right = info_ref[0:1, columns] * (1.0 / LEVELS**2)
    step_right = info_ref[2 if lagged else 1 : 3 if lagged else 2, columns] * weight
    sent_right = lax.rsqrt(info_ref[3:4, columns])
    for index in range(far):
        rows = slice(index * block, (index + 1) * block)
        even = left[2 * index * block : (2 * index + 1) * block]
        odd = left[(2 * index + 1) * block : (2 * index + 2) * block]
        mine = jnp.where(near == 0, even, odd)
        total = keep_ref[rows, :] + from_levels(came_ref[rows, :]) * (mine[:, 0:1] * came_right)
        total = total + mine[:, 1:2] * step_right
        total_ref[index] = total
        level_ref[index] = to_levels(total * (lax.rsqrt(mine[:, 3:4]) * sent_right))
    kept_ref[...] = total_ref[own_far]
    for step, sent_ref in enumerate(sent_refs):
        sent_ref[0:block, :] = level_ref[own_far ^ (step + 1)]


def far_call(counts, keep, came, info, block, lagged):
    half = keep.shape[0]
    far = half // block
    outs = [shape((block, half))]
    outs += [shape((block + (TAIL if lagged else 0), half), jnp.int16)] * (far - 1)
    if lagged:
        outs.append(shape(info.shape))
    estimate = LONG if lagged else SHORT
    return pl.pallas_call(
        functools.partial(far_kernel, lagged=lagged, block=block, far=far),
        in_specs=[WHOLE] * 4,
        out_specs=[WHOLE] * len(outs),
        out_shape=outs,
        scratch_shapes=[
            pltpu.VMEM((far, block, half), jnp.float32),
            pltpu.VMEM((far, block, half), jnp.int16),
        ],
        compiler_params=params(),
        cost_estimate=pl.CostEstimate(flops=estimate, bytes_accessed=estimate // 1024, transcendentals=0),
        name="far_lag" if lagged else "far_zero",
    )(counts, keep, came, info)


def first_last(items):
    return [*items[1:], *items[:1]]


def last_first(items):
    return [*items[-1:], *items[:-1]]


def gathered_total(kept_ref, came_refs, rows_ref, left_ref, columns):
    block, far = kept_ref.shape[0], len(came_refs) + 1
    total = kept_ref[...]
    for index, came_ref in enumerate(came_refs):
        row = 2 * far + index
        right = rows_ref[row : row + 1, columns] * (1.0 / LEVELS**2)
        total = total + from_levels(came_ref[0:block, :]) * (left_ref[:, row : row + 1] * right)
    return total


def finish_lag_kernel(counts_ref, info_ref, kept_ref, *refs, far):
    came_refs = last_first(refs[: far - 1])
    out_ref, zero_ref, rows_ref, left_ref, turned_ref = refs[far - 1 :]
    block, half = kept_ref.shape
    columns = side_columns(half, True)
    found = [decode(came_ref[block : block + TAIL, :]) for came_ref in came_refs]
    rows = [info_ref[4:5, :]] + [f[0] for f in found] + [info_ref[5:6, :]] + [f[1] for f in found]
    rows += [f[2] for f in found]
    rows += [jnp.zeros_like(rows[0])] * (rows_ref.shape[0] - len(rows))
    rows_ref[...] = jnp.concatenate(rows, axis=0)
    turned_ref[...] = jnp.transpose(rows_ref[...])
    first = pl.multiple_of(lax.axis_index("dp") * block, block)
    left_ref[...] = turned_ref[pl.ds(first, block), :]
    pair_total = counts_ref[1:2, 0:1]
    lead_mean = lead_row = lag_row = 0.0
    for k in range(far):
        lead_mean += left_ref[:, k : k + 1]
        lead_row += rows_ref[k : k + 1, columns]
        lag_row += rows_ref[far + k : far + k + 1, columns]
    lead_mean, lead_row, lag_row = (v / pair_total for v in (lead_mean, lead_row, lag_row))
    lag = gathered_total(kept_ref, came_refs, rows_ref, left_ref, columns)
    zero = jnp.zeros_like(lag)
    for k in range(far):
        weight = live_of(counts_ref, [4 * k + i for i in range(4)])
        lead = left_ref[:, k : k + 1] - lead_mean * weight
        zero = zero + lead * (rows_ref[k : k + 1, columns] / weight - lead_row)
        lag = lag + lead * (rows_ref[far + k : far + k + 1, columns] / weight - lag_row)
    out_ref[...] = lag / pair_total
    zero_ref[...] = zero


def finish_lag(counts, info, kept, came):
    block, half = kept.shape
    feats = 2 * half
    far = len(came) + 1
    rows = round_up(3 * far - 1, 8)
    return pl.pallas_call(
        functools.partial(finish_lag_kernel, far=far),
        in_specs=[WHOLE] * (3 + len(came)),
        out_specs=[WHOLE] * 4,
        out_shape=[shape(kept.shape), shape(kept.shape), shape((rows, feats)), shape((block, rows))],
        scratch_shapes=[pltpu.VMEM((feats, rows), jnp.float32)],
        compiler_params=params(),
        name="finish_lag",
    )(counts, info, kept, *first_last(came))


def finish_zero_kernel(counts_ref, rows_ref, left_ref, between_ref, kept_ref, *refs):
    came_refs, out_ref = last_first(refs[:-1]), refs[-1]
    columns = side_columns(kept_ref.shape[1], True)
    zero = gathered_total(kept_ref, came_refs, rows_ref, left_ref, columns)
    out_ref[...] = (zero + between_ref[...]) / counts_ref[1:2, 0:1]


def finish_zero(counts, rows, left, between, kept, came):
    return pl.pallas_call(
        finish_zero_kernel,
        in_specs=[WHOLE] * (5 + len(came)),
        out_specs=WHOLE,
        out_shape=shape(kept.shape),
        compiler_params=params(),
        name="finish_zero",
    )(counts, rows, left, between, kept, *first_last(came))


def exclusive(size, distance):
    return [(i, i ^ distance) for i in range(size)]


def local(coords, lengths, atom_pairs):
    feats = atom_pairs.shape[1]
    dp = lax.axis_size("dp")
    far = dp // 2
    block = feats // dp
    home = coords.shape[0]
    depth = round_up(home - LAG, DEPTH_UNIT)
    rows = round_up(max(home, depth + LAG), FRAME_TILE)

    def swap(array, axis, distance):
        return lax.ppermute(array, axis, exclusive(lax.axis_size(axis), distance))

    coords = pltpu.with_memory_space_constraint(jnp.transpose(coords, (1, 0, 2)), pltpu.HBM)
    atom_pairs = pltpu.with_memory_space_constraint(atom_pairs, pltpu.HBM)
    lengths = pltpu.with_memory_space_constraint(lengths, pltpu.HBM)
    features, stats, sent_lag, counts = contacts_call(coords, lengths, atom_pairs, rows, depth)
    common = [counts, features, stats]
    half = feats // 2
    kept_shape = shape((feats, half))
    came_lag = swap(sent_lag, "tile", 1)
    square = shape((half, half))
    kept_other, right = part_call(
        other_lag_kernel,
        common,
        [sent_lag],
        [square, shape((depth, half), jnp.bfloat16)],
        block,
        LONG,
        "kept_lag_other",
    )
    sent_shape = shape((half + TAIL, half), jnp.int16)
    sent_lag, chip = part_call(
        near_other_kernel,
        [counts, kept_other, stats, came_lag],
        [],
        [sent_shape, shape((8, feats))],
        block,
        SHORT,
        "near_lag_other",
    )
    own_came = came_lag
    came_lag = swap(sent_lag, "dp", 1)
    (kept_own,) = part_call(
        own_lag_kernel, common + [right], [sent_lag], [square], block, SHORT, "kept_lag_own"
    )
    (keep_lag,) = part_call(
        near_own_kernel, [counts, kept_own, chip, own_came], [], [square], block, SHORT, "near_lag_own"
    )
    part_shape = shape((feats // SPLIT, half), jnp.int16)
    sent_zero = gram_call(sent_zero_kernel, common, [keep_lag], [part_shape] * SPLIT, depth, SHORT)
    (kept_zero,) = gram_call(kept_zero_kernel, common, sent_zero[:1], [kept_shape], depth, SHORT)
    came_zero = [swap(part, "tile", 1) for part in sent_zero]
    near_zero = [counts, kept_zero, chip] + came_zero
    (sent_zero,) = part_call(
        functools.partial(near_zero_kernel, own=False),
        near_zero,
        [],
        [shape((half, half), jnp.int16)],
        block,
        SHORT,
        "near_zero_other",
    )
    (keep_zero,) = part_call(
        functools.partial(near_zero_kernel, own=True), near_zero, [], [square], block, SHORT, "near_zero_own"
    )
    came_zero = swap(sent_zero, "dp", 1)

    kept_lag, *sent_lag, pair = far_call(counts, keep_lag, came_lag, chip, block, True)
    came_lag = [swap(s, "dp", 2 * (i + 1)) for i, s in enumerate(sent_lag)]
    kept_zero, *sent_zero = far_call(counts, keep_zero, came_zero, pair, block, False)
    came_zero = [swap(s, "dp", 2 * (i + 1)) for i, s in enumerate(sent_zero)]
    cov_lag, between, total_rows, total_left = finish_lag(counts, pair, kept_lag, came_lag)
    cov_zero = finish_zero(counts, total_rows, total_left, between, kept_zero, came_zero)
    return (cov_zero, cov_lag)


def solution(mesh):
    placed = (P(("groups", "dp", "tile"), None, None), P("groups"), P())
    return jax.shard_map(
        local,
        mesh=mesh,
        in_specs=placed,
        out_specs=(P(("groups", "dp"), "tile"), P(("groups", "dp"), "tile")),
        check_vma=False,
    )
```
